32 devices in a mesh: group: 1, ctx: 16 (over z, y, x), head: 2 (over core).
Axes of the slice: x: 2, y: 2, z: 4, core: 2. Of those that a mesh axis runs over, the one named last changes fastest.
Arguments:
- pair_raw: bfloat16 [4096, 2, 1024], P(('group', 'ctx'), None, 'head'), may hold values from -6 to 6
- value_raw: bfloat16 [4096, 2048], P(('group', 'ctx'), 'head'), may hold values from -6 to 6
- gate_raw: bfloat16 [4096, 2048], P(('group', 'ctx'), 'head'), may hold values from -6 to 6
- write_strength: float32 [4096, 16], P(('group', 'ctx'), 'head'), may hold values from 0.05 to 0.95
- log_decay: float32 [4096, 16], P(('group', 'ctx'), 'head'), may hold values from -2.6 to 0
- segment_ids: int32 [4096], P('group'), may hold values from 0 to 1, never falling along the last dimension, each value on 1 to 3968 neighbouring positions
- pair_filter: float32 [4, 2, 1024], P(None, None, 'head'), may hold values from -3 to 3
- value_filter: float32 [4, 2048], P(None, 'head'), may hold values from -3 to 3
- norm_gain: float32 [128], replicated, may hold values from 0.1 to 1.9
- out_weight: bfloat16 [2048, 2048], P('head'), may hold values from -0.125 to 0.125
- residual: bfloat16 [4096, 2048], P(('group', 'ctx', 'head')), may hold values from -27 to 27
- post_gain: float32 [2048], replicated, may hold values from 0.1 to 1.9
- routes: int32 [4096, 10], P(('group', 'ctx', 'head')), may hold values from 0 to 31, all different within a row; in each aligned block of 128 rows (0 to 127, 128 to 255, ...) at most 50 rows name the same one
- route_weights: float32 [4096, 10], P(('group', 'ctx', 'head')), may hold values from 0.05 to 0.3
- expert_up: bfloat16 [32, 2048, 1024], P(('ctx', 'head')), may hold values from -0.125 to 0.125
- expert_down: bfloat16 [32, 512, 2048], P(('ctx', 'head')), may hold values from -0.25 to 0.25
Outputs:
- layer_out: bfloat16 [4096, 2048], P(('group', 'ctx', 'head'))
The draws below stay inside these ranges and needn't reach their ends.
Inputs may be any that keep to these rules, and one draw needn't show every extreme that they name: `routes`: in each aligned block of 128 rows (the rows of one device) no expert is named by more than 50 rows; a row names 10 different experts. `segment_ids`: rollout numbers never fall along the slab; a rollout holds 1 to 3968 tokens of the slab.
All inputs are finite; a program needn't handle non-finite values.
Results may differ from the reference program's by a relative error of at most 0.012.
Values may be sent and summed in bfloat16 or wider, within the bound.
A program may use at most 128 MiB of HBM per device.

```python
import math
import jax
import jax.numpy as jnp
import numpy as np
from jax import lax

D = 2048
HK = 8
VALUE_HEADS = 16
DK = 128
DV = 128
FFE = 512
TOPK = 10
KW = 4
BLOCK = 64
SEGS = 2
TOK_CTX = 256
SLAB_TOKENS = 4096
TOK_DEV = 128
EXPERTS = 32
CAP = 50
SEG_MOST = 3968
N_CTX = 16
N_HEAD = 2


def draw_log_decay(key, part):
    key_sequence = jax.random.split(jax.random.fold_in(key, 11), 7)
    fast_share = 0.5
    fast_heads = jax.random.uniform(key_sequence[0], (VALUE_HEADS,)) < fast_share
    fast_rate = jax.random.uniform(key_sequence[1], (VALUE_HEADS,), minval=0.08, maxval=0.15)
    slow_rate = 0.3 / SLAB_TOKENS * jax.random.uniform(key_sequence[2], (VALUE_HEADS,), minval=0.5, maxval=1.0)
    head_decay_rate = jnp.where(fast_heads, fast_rate, slow_rate)
    block_count = SLAB_TOKENS // TOK_CTX
    block_multiplier = jnp.exp(jax.random.uniform(key_sequence[3], (block_count, 1, VALUE_HEADS), minval=math.log(0.5), maxval=math.log(2.0)))
    block_multiplier = jnp.broadcast_to(block_multiplier, (block_count, TOK_CTX, VALUE_HEADS)).reshape(SLAB_TOKENS, VALUE_HEADS)
    element_multiplier = jnp.exp(jax.random.uniform(key_sequence[4], (SLAB_TOKENS, VALUE_HEADS), minval=math.log(0.7), maxval=math.log(1.4)))
    spike_position = jax.random.randint(key_sequence[5], (3,), 0, SLAB_TOKENS)
    spike_penalty = jax.random.uniform(key_sequence[6], (3, VALUE_HEADS), minval=0.2, maxval=0.5)
    token_positions = jnp.arange(SLAB_TOKENS)
    match_count = (token_positions[None, :, None] == spike_position[:, None, None]).astype(jnp.float32)
    spike_events = jnp.sum(match_count * jnp.log1p(-spike_penalty)[:, None, :], axis=0)
    return (-head_decay_rate[None, :] * block_multiplier * element_multiplier + spike_events).astype(jnp.float32)


def draw_residual(key, part):
    key_sequence = jax.random.split(jax.random.fold_in(key, 23), 3)
    row_scale = jnp.exp(jax.random.uniform(key_sequence[0], (SLAB_TOKENS, 1), minval=0.0, maxval=math.log(10.0))) / 3.0
    col_scale = jnp.exp(jax.random.uniform(key_sequence[1], (1, D), minval=math.log(0.5), maxval=math.log(2.0)))
    base = jnp.clip(jax.random.normal(key_sequence[2], (SLAB_TOKENS, D)), -4.0, 4.0)
    return (base * row_scale * col_scale).astype(jnp.bfloat16)


def block_scale(key, shape, cuts, smallest, top_value):
    def one(axis_at, blocks):
        draws = jax.random.uniform(jax.random.fold_in(jax.random.fold_in(key, 6), axis_at), (blocks,), jnp.float32, smallest / len(cuts), top_value / len(cuts))
        return jnp.repeat(jnp.exp(draws), shape[axis_at] // blocks).reshape((-1,) + (1,) * (len(shape) - axis_at - 1))

    factor_of = one(*cuts[0])
    for cut in cuts[1:]:
        factor_of = factor_of * one(*cut)
    return factor_of


def profile(amount, total, limit, lean):
    weights = [(1 << 20) // math.isqrt(rank ** lean) + 1 for rank in range(2, amount + 1)]
    spare, holding = total - limit - (amount - 1), [1] * (amount - 1)
    while spare > 0:
        free = [i for i in range(amount - 1) if holding[i] < limit]
        pool, budget = sum([weights[i] for i in free]), spare
        for i in free:
            addition = min(limit - holding[i], max(1, budget * weights[i] // pool), spare)
            holding[i] = holding[i] + addition
            spare = spare - addition
    return np.array([limit] + holding)


def ragged(own_key, amount, total, reach, lean):
    if amount == 2:
        one = jax.random.randint(own_key, (), max(1, total - reach), min(reach, total - 1) + 1)
        return jnp.stack([one, total - one])
    sizes = jnp.asarray(profile(amount, total, reach, lean), jnp.int32)
    pairs = (amount - 1) // 2
    donor, sink = sizes[1:1 + 2 * pairs:2], sizes[2:2 + 2 * pairs:2]
    room = jnp.minimum(donor - 1, reach - sink)
    moved = jax.random.randint(jax.random.fold_in(own_key, 1), (pairs,), 0, 1 << 20) % (room + 1)
    sizes = sizes.at[1:1 + 2 * pairs:2].set(donor - moved).at[2:2 + 2 * pairs:2].set(sink + moved)
    return sizes[jax.random.permutation(jax.random.fold_in(own_key, 2), amount)]


def shared_out(key, own, number, rows, amount, top, bound, lean):
    sequence = jax.random.permutation(key, amount)
    packed, usual = portions_of(amount, rows * top, bound, lean, True), portions_of(amount, rows * top, bound, lean, False)
    places = jnp.arange(amount)

    def named(sizes, offset_by):
        used = int((sizes > 0).sum())
        fixed = max(1, used // 4)
        moved = fixed + (places - fixed + offset_by * (used - fixed)) % max(1, amount - fixed)
        return jnp.zeros((amount,), jnp.int32).at[sequence[jnp.where(places < fixed, places, moved)]].set(jnp.asarray(sizes, jnp.int32))

    sizes = jnp.where(number % 4 == 0, named(packed, number // 4), named(usual, number - number // 4 - 1))
    mixed = jax.random.permutation(jax.random.fold_in(own, 3), amount)
    source_of, taker = mixed[0:amount // 2 * 2:2], mixed[1:amount // 2 * 2:2]
    slack = jnp.minimum(sizes[source_of] - 1, bound - sizes[taker]) // 2
    slack = jnp.where((source_of == sequence[0]) | (taker == sequence[0]) | (sizes[taker] == 0), 0, jnp.maximum(slack, 0))
    moved = jax.random.randint(jax.random.fold_in(own, 4), (amount // 2,), 0, 1 << 20) % (slack + 1)
    sizes = sizes.at[source_of].add(-moved).at[taker].add(moved)
    members = jnp.searchsorted(jnp.cumsum(sizes), jnp.arange(rows * top), side="right").astype(jnp.int32)
    table = members.reshape(top, rows).T
    table = table[jax.random.permutation(jax.random.fold_in(own, 1), rows)]
    offset_by = jax.random.randint(jax.random.fold_in(own, 2), (rows, 1), 0, top)
    return jnp.take_along_axis(table, (jnp.arange(top)[None, :] + offset_by) % top, axis=1)


def portions_of(number_of, total, limit, slope, full):
    portions = [(1 << 20) // math.isqrt(rank ** slope) + 1 for rank in range(1, number_of + 1)]
    largest = limit if full else min(limit, max(-(-total // number_of), total * portions[0] // sum(portions)))
    least = 1 if total - largest >= number_of - 1 else 0
    counts, surplus = [largest] + [least] * (number_of - 1), total - largest - least * (number_of - 1)
    while surplus > 0:
        free = [i for i in range(1, number_of) if counts[i] < largest] or [i for i in range(1, number_of) if counts[i] < limit]
        whole, budget = sum([portions[i] for i in free]), surplus
        for i in free:
            more = min(limit - counts[i], max(1, budget * portions[i] // whole), surplus)
            counts[i] = counts[i] + more
            surplus = surplus - more
    return np.array(counts)


def gaussian(own_key, shape, spread, bound, cuts=(), held_as=jnp.bfloat16):
    entries = jax.random.normal(own_key, shape, jnp.float32) * spread
    if len(cuts) > 0:
        entries = block_scale(own_key, shape, cuts, -0.22, 0.18) * entries
    return jnp.clip(entries, min=-bound, max=bound).astype(held_as)


def setup_inputs(seed: int = 0, part: int = 0) -> dict:
    arg_keys = jax.random.split(jax.random.key(seed), 17)
    part_keys = jax.random.split(jax.random.fold_in(arg_keys[16], part), 17)
    pair_raw = gaussian(part_keys[0], (SLAB_TOKENS, 2, HK * DK), 1.0, 6.0, ((0, 16), (2, 2)))
    value_raw = gaussian(part_keys[1], (SLAB_TOKENS, VALUE_HEADS * DV), 1.0, 6.0, ((0, 16), (1, 2)))
    gate_raw = gaussian(part_keys[2], (SLAB_TOKENS, VALUE_HEADS * DV), 1.0, 6.0, ((0, 16), (1, 2)))
    write_strength = jnp.clip(0.05 + 0.9 * jax.random.uniform(part_keys[3], (SLAB_TOKENS, VALUE_HEADS), jnp.float32) ** block_scale(part_keys[3], (SLAB_TOKENS, VALUE_HEADS), ((0, 16), (1, 2)), -0.2, 0.2), 0.05, 0.95)
    log_decay = draw_log_decay(jax.random.fold_in(jax.random.fold_in(arg_keys[16], part), 71), part)
    segment_ids = jnp.searchsorted(jnp.cumsum(ragged(part_keys[5], SEGS, SLAB_TOKENS, SEG_MOST, 1)), jnp.arange(SLAB_TOKENS), side="right").astype(jnp.int32)
    pair_filter = gaussian(arg_keys[6], (KW, 2, HK * DK), KW ** -0.5, 3.0, ((2, 2),), jnp.float32)
    value_filter = gaussian(arg_keys[7], (KW, VALUE_HEADS * DV), KW ** -0.5, 3.0, ((1, 2),), jnp.float32)
    norm_gain = jnp.clip(1.0 + 0.18 * jax.random.normal(arg_keys[8], (DV,), jnp.float32), 0.1, 1.9)
    out_weight = gaussian(arg_keys[9], (VALUE_HEADS * DV, D), (VALUE_HEADS * DV) ** -0.5, 0.125, ((0, 2),))
    residual = draw_residual(jax.random.fold_in(jax.random.fold_in(arg_keys[16], part), 71), part)
    post_gain = jnp.clip(1.0 + 0.18 * jax.random.normal(arg_keys[11], (D,), jnp.float32), 0.1, 1.9)
    routes_keys = jax.random.split(jax.random.fold_in(part_keys[12], 1), SLAB_TOKENS // TOK_DEV)
    routes_turns = jax.random.permutation(jax.random.fold_in(part_keys[12], 3), SLAB_TOKENS // TOK_DEV)
    routes = jax.vmap(lambda own, number: shared_out(jax.random.fold_in(part_keys[12], 2), own, number, TOK_DEV, EXPERTS, TOPK, CAP, 2))(routes_keys, routes_turns).reshape((SLAB_TOKENS, TOPK))
    route_weights = jnp.clip(0.05 + 0.25 * jax.random.uniform(part_keys[13], (SLAB_TOKENS, TOPK), jnp.float32) ** block_scale(part_keys[13], (SLAB_TOKENS, TOPK), ((0, 32),), -0.2, 0.2), 0.05, 0.3)
    expert_up = gaussian(arg_keys[14], (EXPERTS, D, 2 * FFE), D ** -0.5, 0.125, ((0, 32),))
    expert_down = gaussian(arg_keys[15], (EXPERTS, FFE, D), FFE ** -0.5, 0.25, ((0, 32),))
    return dict(pair_raw=pair_raw, value_raw=value_raw, gate_raw=gate_raw, write_strength=write_strength, log_decay=log_decay, segment_ids=segment_ids, pair_filter=pair_filter, value_filter=value_filter, norm_gain=norm_gain, out_weight=out_weight, residual=residual, post_gain=post_gain, routes=routes, route_weights=route_weights, expert_up=expert_up, expert_down=expert_down)


HIGHEST = lax.Precision.HIGHEST

def precise_dot(left, right):
    return jnp.dot(left.astype(jnp.float32), right.astype(jnp.float32), precision=HIGHEST, preferred_element_type=jnp.float32)

def causal_filter(padded_raw, filter_taps, padded_ids, kernel):
    length = padded_raw.shape[0] - (kernel - 1)
    source = padded_raw.astype(jnp.float32)
    current_ids = padded_ids[kernel - 1:]
    summed = jnp.zeros((length, padded_raw.shape[1]), jnp.float32)
    for lag_step in range(kernel):
        offset_start = kernel - 1 - lag_step
        shifted = source[offset_start:offset_start + length]
        matching = (padded_ids[offset_start:offset_start + length] == current_ids).astype(jnp.float32)
        summed = summed + filter_taps[lag_step] * shifted * matching[:, None]
    return jax.nn.silu(summed)

def unit_rows(values_in):
    return values_in / jnp.sqrt(lax.optimization_barrier(jnp.sum(values_in * values_in, axis=-1, keepdims=True)) + 1e-06)

def mixer_inputs(pair_padded, value_padded, pair_filter, value_filter, padded_ids, kernel):
    pair_act = causal_filter(pair_padded, pair_filter.reshape(kernel, -1), padded_ids, kernel)
    length = pair_act.shape[0]
    pair_heads = pair_act.reshape(length, 2, -1, DK)
    queries = unit_rows(pair_heads[:, 0]) * DK ** (-0.5)
    key_rows = unit_rows(pair_heads[:, 1])
    value_rows = causal_filter(value_padded, value_filter, padded_ids, kernel).reshape(length, -1, DV)
    repeat_factor = value_rows.shape[1] // key_rows.shape[1]
    return (jnp.repeat(queries, repeat_factor, axis=1), jnp.repeat(key_rows, repeat_factor, axis=1), value_rows)

def block_setup(queries, key_rows, value_rows, strength, decay_rows, segment_here, prior_id):
    cumulative = jnp.cumsum(decay_rows)
    row_index = lax.broadcasted_iota(jnp.int32, (BLOCK, BLOCK), 0)
    col_index = lax.broadcasted_iota(jnp.int32, (BLOCK, BLOCK), 1)
    same_segment = segment_here[:, None] == segment_here[None, :]
    causal = (row_index >= col_index) & same_segment
    strictly = (row_index > col_index) & same_segment
    decay_matrix = jnp.where(causal, jnp.exp(jnp.where(causal, cumulative[:, None] - cumulative[None, :], 0.0)), 0.0)
    carried_in = (segment_here == prior_id).astype(jnp.float32)
    keyed_beta = key_rows * strength[:, None]
    coupling = jnp.where(strictly, precise_dot(keyed_beta, key_rows.T) * decay_matrix, 0.0)
    system = jnp.eye(BLOCK, dtype=jnp.float32) + coupling
    stacked = jnp.concatenate([value_rows * strength[:, None], keyed_beta * (jnp.exp(cumulative) * carried_in)[:, None]], axis=1)
    solved = lax.linalg.triangular_solve(system, stacked, left_side=True, lower=True, unit_diagonal=True)
    targets = solved[:, :DV]
    corrector = solved[:, DV:]
    within = jnp.where(causal, precise_dot(queries, key_rows.T) * decay_matrix, 0.0)
    query_decayed = queries * (jnp.exp(cumulative) * carried_in)[:, None]
    final_log = cumulative[BLOCK - 1]
    weighting = (segment_here == segment_here[BLOCK - 1]).astype(jnp.float32) * jnp.exp(final_log - cumulative)
    keys_weighted = key_rows * weighting[:, None]
    transition = jnp.exp(final_log) * carried_in[BLOCK - 1] * jnp.eye(DK, dtype=jnp.float32) - precise_dot(keys_weighted.T, corrector)
    increment = precise_dot(keys_weighted.T, targets)
    return (within, query_decayed, targets, corrector, transition, increment)

def head_major(array_in, block_count):
    moved = jnp.moveaxis(array_in, 1, 0)
    return moved.reshape((array_in.shape[1], block_count, BLOCK) + array_in.shape[2:])

def block_tables(queries, key_rows, value_rows, strength, decay_rows, padded_ids, kernel):
    length = queries.shape[0]
    block_count = length // BLOCK
    current_ids = padded_ids[kernel - 1:].reshape(block_count, BLOCK)
    prior_ids = padded_ids[kernel - 2:kernel - 2 + length:BLOCK]
    per_block = jax.vmap(block_setup, in_axes=(0, 0, 0, 0, 0, 0, 0))
    per_head = jax.vmap(per_block, in_axes=(0, 0, 0, 0, 0, None, None))
    return per_head(head_major(queries, block_count), head_major(key_rows, block_count), head_major(value_rows, block_count), head_major(strength, block_count), head_major(decay_rows, block_count), current_ids, prior_ids)

def batched(left, right):
    return jnp.einsum('hij,hjk->hik', left, right, precision=HIGHEST)

def sweep_blocks(block_terms, start_state):
    blocks_first = tuple((jnp.swapaxes(member, 0, 1) for member in block_terms))

    def advance(carry_state, pieces):
        within, query_decayed, targets, corrector, transition, increment = pieces
        fresh_values = targets - batched(corrector, carry_state)
        emitted = batched(query_decayed, carry_state) + batched(within, fresh_values)
        updated = batched(transition, carry_state) + increment
        return (updated, emitted)
    final_state, emitted = lax.scan(advance, start_state, blocks_first)
    return emitted

def tokens_first(emitted):
    heads_count = emitted.shape[1]
    return jnp.transpose(emitted, (0, 2, 1, 3)).reshape(-1, heads_count, emitted.shape[3])

def gate_output(mixed_heads, gate_raw, norm_gain):
    square_mean = lax.optimization_barrier(jnp.mean(mixed_heads * mixed_heads, axis=-1, keepdims=True))
    gate_values = jax.nn.silu(gate_raw.reshape(mixed_heads.shape).astype(jnp.float32))
    normed = mixed_heads / jnp.sqrt(square_mean + 1e-06) * norm_gain * gate_values
    return normed.astype(jnp.bfloat16).reshape(mixed_heads.shape[0], -1)

def post_norm(hidden, post_gain):
    hidden_full = hidden.astype(jnp.float32)
    square_mean = lax.optimization_barrier(jnp.mean(hidden_full * hidden_full, axis=-1, keepdims=True))
    return (hidden_full / jnp.sqrt(square_mean + 1e-06) * post_gain).astype(jnp.bfloat16)

def expert_apply_rows(rows_in, up_matrix, down_matrix):
    hidden_units = down_matrix.shape[0]
    gate_up = jnp.dot(rows_in.astype(jnp.float32), up_matrix.astype(jnp.float32), preferred_element_type=jnp.float32)
    activated = (jax.nn.silu(gate_up[:, :hidden_units]) * gate_up[:, hidden_units:]).astype(jnp.bfloat16)
    return jnp.dot(activated.astype(jnp.float32), down_matrix.astype(jnp.float32), preferred_element_type=jnp.float32).astype(jnp.bfloat16)

def reference(pair_raw, value_raw, gate_raw, write_strength, log_decay, segment_ids, pair_filter, value_filter, norm_gain, out_weight, residual, post_gain, routes, route_weights, expert_up, expert_down):
    kernel = value_filter.shape[0]
    padded_ids = jnp.concatenate([jnp.full((kernel - 1,), -1, jnp.int32), segment_ids.astype(jnp.int32)])
    pair_flat = pair_raw.reshape(SLAB_TOKENS, -1)
    pair_padded = jnp.concatenate([jnp.zeros((kernel - 1, pair_flat.shape[1]), jnp.bfloat16), pair_flat])
    value_padded = jnp.concatenate([jnp.zeros((kernel - 1, value_raw.shape[1]), jnp.bfloat16), value_raw])
    queries, key_rows, value_rows = mixer_inputs(pair_padded, value_padded, pair_filter, value_filter, padded_ids, kernel)
    block_terms = block_tables(queries, key_rows, value_rows, write_strength, log_decay, padded_ids, kernel)
    start_state = jnp.zeros((VALUE_HEADS, DK, DV), jnp.float32)
    emitted = sweep_blocks(block_terms, start_state)
    gated_out = gate_output(tokens_first(emitted), gate_raw, norm_gain)
    attention = jnp.dot(gated_out.astype(jnp.float32), out_weight.astype(jnp.float32), preferred_element_type=jnp.float32)
    hidden = (residual.astype(jnp.float32) + attention).astype(jnp.bfloat16)
    expert_in = post_norm(hidden, post_gain)
    blocks = N_CTX * N_HEAD
    rows_each = SLAB_TOKENS // blocks
    assigned = routes.reshape(blocks, rows_each * TOPK)
    expert_ids = jnp.arange(EXPERTS, dtype=jnp.int32)
    onehot = (assigned[:, :, None] == expert_ids[None, None, :]).astype(jnp.int32)
    slot_rank = lax.optimization_barrier(jnp.sum((jnp.cumsum(onehot, axis=1) - 1) * onehot, axis=2))
    source_ids = jnp.arange(blocks, dtype=jnp.int32)[:, None]
    slot_index = assigned * (blocks * CAP) + source_ids * CAP + slot_rank
    owners = jnp.arange(blocks * rows_each * TOPK, dtype=jnp.int32) // TOPK + 1
    owner_table = jnp.zeros((EXPERTS * blocks * CAP,), jnp.int32).at[slot_index.reshape(-1)].set(owners)

    def one_expert(operands):
        table_row, up_matrix, down_matrix = operands
        picked = jnp.where((table_row > 0)[:, None], expert_in[jnp.maximum(table_row - 1, 0)], jnp.zeros((), jnp.bfloat16))
        return expert_apply_rows(picked, up_matrix, down_matrix)
    results = lax.map(one_expert, (owner_table.reshape(EXPERTS, blocks * CAP), expert_up, expert_down)).reshape(-1, D)
    chosen_slots = slot_index.reshape(SLAB_TOKENS, TOPK)
    combined = hidden.astype(jnp.float32)
    for column in range(TOPK):
        combined = combined + route_weights[:, column:column + 1] * results[chosen_slots[:, column]].astype(jnp.float32)
    return combined.astype(jnp.bfloat16)
```

```python
import functools

import jax
import jax.numpy as jnp
from jax import lax
from jax.experimental import pallas as pl
from jax.experimental.pallas import tpu as pltpu
from jax.sharding import PartitionSpec as P

DK = 128
DV = 128
PAD = 16
EPS = 1e-06
NN = (((1,), (0,)), ((), ()))
NT = (((1,), (1,)), ((), ()))
TN = (((0,), (0,)), ((), ()))
VMEM_MOST = 56 * 1024 * 1024


def dot16(left, right, dims=NN):
    return lax.dot_general(
        left.astype(jnp.bfloat16),
        right.astype(jnp.bfloat16),
        dims,
        preferred_element_type=jnp.float32,
    )


def halves(x):
    high = x.astype(jnp.bfloat16)
    return high, (x - high.astype(jnp.float32)).astype(jnp.bfloat16)


def dot_split(left, right, dims=NN):
    lh, ll = halves(left)
    rh, rl = halves(right)
    return dot16(lh, rh, dims) + (dot16(lh, rl, dims) + dot16(ll, rh, dims))


def silu(x):
    return x * (1.0 / (1.0 + jnp.exp(-x)))


def filtered(raw_ref, taps_ref, match, lanes):
    rows = raw_ref.shape[0] - PAD
    source = raw_ref[:, lanes].astype(jnp.float32)
    taps = taps_ref[:, lanes]
    total = taps[0:1] * source[PAD:]
    for lag in range(1, taps_ref.shape[0]):
        total = total + taps[lag : lag + 1] * (source[PAD - lag : PAD - lag + rows] * match[lag])
    return silu(total)


def unit_rows(x):
    return x * lax.rsqrt(jnp.sum(x * x, axis=-1, keepdims=True) + EPS)


def inverse_unit_lower(coupling, row, col):
    size = coupling.shape[0]
    apart = row ^ col
    inverse = jnp.where(row == col, 1.0, 0.0) - jnp.where(apart == 1, coupling, 0.0)
    step = 2
    while step < size:
        cross = jnp.where((apart >= step) & (apart < 2 * step), coupling, 0.0)
        inverse = inverse - dot16(inverse, dot16(cross, inverse))
        step *= 2
    return inverse


def local_kernel(
    q_ref, k_ref, v_ref, qt_ref, kt_ref, vt_ref, seg_ref, segrow_ref,
    cum_ref, cumrow_ref, beta_ref, qeff_ref, off_ref, maps_ref,
):
    rows = qeff_ref.shape[1]
    seg = seg_ref[...]
    match = [None] + [(seg[:, lag : lag + 1] == seg[:, 0:1]).astype(jnp.float32) for lag in range(1, 4)]
    ids = seg[:, 0:1]
    carried = (ids == seg_ref[0:1, 1:2]).astype(jnp.float32)
    at_end = (ids == seg_ref[rows - 1 : rows, 0:1]).astype(jnp.float32)
    row = lax.broadcasted_iota(jnp.int32, (rows, rows), 0)
    col = lax.broadcasted_iota(jnp.int32, (rows, rows), 1)
    same = ids == segrow_ref[...]
    causal = (row >= col) & same
    strictly = (row > col) & same
    queries = unit_rows(filtered(q_ref, qt_ref, match, slice(None))) * DK ** (-0.5)
    keys = unit_rows(filtered(k_ref, kt_ref, match, slice(None)))
    q16 = queries.astype(jnp.bfloat16)
    k16 = keys.astype(jnp.bfloat16)
    gram = dot16(k16, k16, NT)
    cross = dot16(q16, k16, NT)
    k32 = k16.astype(jnp.float32)
    q32 = q16.astype(jnp.float32)
    eye = (
        lax.broadcasted_iota(jnp.int32, (DK, DK), 0) == lax.broadcasted_iota(jnp.int32, (DK, DK), 1)
    ).astype(jnp.float32)
    for member in range(qeff_ref.shape[0]):
        lanes = slice(member * DV, (member + 1) * DV)
        values = filtered(v_ref, vt_ref, match, lanes)
        cum = cum_ref[member]
        beta = beta_ref[member]
        decay = jnp.exp(jnp.where(causal, cum - cumrow_ref[member], 0.0))
        coupling = jnp.where(strictly, gram * decay * beta, 0.0)
        within = jnp.where(causal, cross * decay, 0.0)
        grown = jnp.exp(cum) * carried
        inverse = inverse_unit_lower(coupling, row, col)
        stacked = jnp.concatenate([values * beta, k32 * (beta * grown)], axis=1)
        solved = dot16(inverse, stacked)
        both = dot16(within, solved)
        off_ref[member] = both[:, :DV]
        qeff_ref[member] = (q32 * grown - both[:, DV:]).astype(jnp.bfloat16)
        final = cum[rows - 1 : rows]
        weighted = k32 * (at_end * jnp.exp(final - cum))
        sums = dot16(solved, weighted, TN)
        shift_t = sums[:DV]
        forward = (jnp.exp(final) * carried[rows - 1 : rows]) * eye - sums[DV:].T
        for half in range(2):
            at = member * 2 + half
            maps_ref[at, :DK, :] = forward.astype(jnp.bfloat16)
            maps_ref[at, DK:, :] = shift_t[half * (DV // 2) : (half + 1) * (DV // 2)].astype(jnp.bfloat16)


def local_maps(pair, value, pair_taps, value_taps, seg, segrow, cum, cumrow, beta):
    heads, rows = beta.shape[:2]
    key_heads = pair.shape[1] // (2 * DK)
    per = heads // key_heads
    padded = pair.shape[0]
    taps = pair_taps.shape[0]
    whole = lambda g: (0, 0)
    return pl.pallas_call(
        local_kernel,
        grid=(key_heads,),
        in_specs=[
            pl.BlockSpec((padded, DK), lambda g: (0, g)),
            pl.BlockSpec((padded, DK), lambda g: (0, key_heads + g)),
            pl.BlockSpec((padded, per * DV), lambda g: (0, g)),
            pl.BlockSpec((taps, DK), lambda g: (0, g)),
            pl.BlockSpec((taps, DK), lambda g: (0, key_heads + g)),
            pl.BlockSpec((taps, per * DV), lambda g: (0, g)),
            pl.BlockSpec((rows, taps), whole),
            pl.BlockSpec((1, rows), whole),
            pl.BlockSpec((per, rows, 1), lambda g: (g, 0, 0)),
            pl.BlockSpec((per, 1, rows), lambda g: (g, 0, 0)),
            pl.BlockSpec((per, rows, 1), lambda g: (g, 0, 0)),
        ],
        out_specs=[
            pl.BlockSpec((per, rows, DK), lambda g: (g, 0, 0)),
            pl.BlockSpec((per, rows, DV), lambda g: (g, 0, 0)),
            pl.BlockSpec((2 * per, DK + DV // 2, DK), lambda g: (g, 0, 0)),
        ],
        out_shape=[
            jax.ShapeDtypeStruct((heads, rows, DK), jnp.bfloat16),
            jax.ShapeDtypeStruct((heads, rows, DV), jnp.float32),
            jax.ShapeDtypeStruct((2 * heads, DK + DV // 2, DK), jnp.bfloat16),
        ],
        compiler_params=pltpu.CompilerParams(vmem_limit_bytes=VMEM_MOST),
        name="local_maps",
    )(pair, pair, value, pair_taps, pair_taps, value_taps, seg, segrow, cum, cumrow, beta)


def carry_kernel(maps_ref, states_ref):
    state = jnp.zeros(states_ref.shape[1:], jnp.float32)
    for at in range(maps_ref.shape[0]):
        states_ref[at] = state.astype(jnp.bfloat16)
        if at + 1 < maps_ref.shape[0]:
            moved = dot16(state, maps_ref[at, :DK, :], NT)
            state = moved + maps_ref[at, DK:, :].astype(jnp.float32)


def carried_states(maps):
    peers = maps.shape[0]
    return pl.pallas_call(
        carry_kernel,
        out_shape=jax.ShapeDtypeStruct((peers, DV // 2, DK), jnp.bfloat16),
        compiler_params=pltpu.CompilerParams(vmem_limit_bytes=VMEM_MOST),
        name="carried_states",
    )(maps)


def emit_kernel(qeff_ref, off_ref, state_ref, gate_ref, gain_ref, weight_ref, out_ref, gated_ref):
    heads = qeff_ref.shape[0]
    gain = gain_ref[...]
    for head in range(heads):
        lanes = slice(head * DV, (head + 1) * DV)
        mixed = off_ref[head] + dot16(qeff_ref[head], state_ref[head], NT)
        scale = lax.rsqrt(jnp.mean(mixed * mixed, axis=-1, keepdims=True) + EPS)
        gate = silu(gate_ref[:, lanes].astype(jnp.float32))
        gated_ref[:, lanes] = (mixed * scale * gain * gate).astype(jnp.bfloat16)
    width = out_ref.shape[1]
    tile = 512
    for at in range(0, width, tile):
        out_ref[:, at : at + tile] = jnp.dot(
            gated_ref[...], weight_ref[:, at : at + tile], preferred_element_type=jnp.float32
        )


def emitted_rows(qeff, off, states, gate_raw, gain, weight):
    rows, channels = gate_raw.shape
    return pl.pallas_call(
        emit_kernel,
        out_shape=jax.ShapeDtypeStruct((rows, weight.shape[1]), jnp.float32),
        scratch_shapes=[pltpu.VMEM((rows, channels), jnp.bfloat16)],
        compiler_params=pltpu.CompilerParams(vmem_limit_bytes=VMEM_MOST),
        name="emitted_rows",
    )(qeff, off, states, gate_raw, gain, weight)


def mixer(
    pair_raw, value_raw, gate_raw, write_strength, log_decay, segment_ids,
    pair_filter, value_filter, norm_gain, out_weight,
):
    rows = pair_raw.shape[0]
    taps = value_filter.shape[0]
    peers = lax.axis_size("ctx")
    pair = pair_raw.reshape(rows, -1)
    width = pair.shape[1]
    rim = jnp.concatenate([pair[rows - PAD :], value_raw[rows - PAD :]], axis=1)
    before = lax.ppermute(rim, "ctx", [(i, i + 1) for i in range(peers - 1)])
    first = lax.axis_index("ctx") * rows
    padded_ids = jnp.concatenate([jnp.full((taps - 1,), -1, jnp.int32), segment_ids])
    ids = lax.dynamic_slice_in_dim(padded_ids, first, rows + taps - 1)
    seg = jnp.stack([ids[taps - 1 - lag : taps - 1 - lag + rows] for lag in range(taps)], axis=1)
    segrow = ids[taps - 1 :][None, :]
    cum = jnp.cumsum(log_decay, axis=0).T
    qeff, off, maps = local_maps(
        jnp.concatenate([before[:, :width], pair]),
        jnp.concatenate([before[:, width:], value_raw]),
        pair_filter.reshape(taps, -1),
        value_filter,
        seg,
        segrow,
        cum[:, :, None],
        cum[:, None, :],
        write_strength.T[:, :, None],
    )
    heads = qeff.shape[0]
    arrived = lax.all_to_all(maps, "ctx", split_axis=0, concat_axis=0, tiled=True)
    states = lax.all_to_all(carried_states(arrived), "ctx", split_axis=0, concat_axis=0, tiled=True)
    states = states.reshape(heads, DV, DK)
    return emitted_rows(qeff, off, states, gate_raw, norm_gain[None, :], out_weight)


def post_norm(hidden, post_gain):
    hidden_full = hidden.astype(jnp.float32)
    square_mean = jnp.mean(hidden_full * hidden_full, axis=-1, keepdims=True)
    return (hidden_full / jnp.sqrt(square_mean + 1e-06) * post_gain).astype(jnp.bfloat16)


def expert_apply_rows(rows_in, up_matrix, down_matrix):
    hidden_units = down_matrix.shape[0]
    gate_up = jnp.dot(rows_in, up_matrix, preferred_element_type=jnp.float32)
    activated = (jax.nn.silu(gate_up[:, :hidden_units]) * gate_up[:, hidden_units:]).astype(
        jnp.bfloat16
    )
    return jnp.dot(activated, down_matrix, preferred_element_type=jnp.float32).astype(jnp.bfloat16)


def expert_apply(arrived, expert_up, expert_down):
    member_rows = arrived[:, 0]
    flattened = member_rows.reshape(-1, member_rows.shape[-1])
    result = expert_apply_rows(flattened, expert_up[0], expert_down[0])
    outputs = [result.reshape(member_rows.shape)]
    return jnp.stack(outputs, axis=1)


def route_slots(routes, experts_all, capacity):
    assigned = routes.reshape(-1)
    expert_ids = jnp.arange(experts_all, dtype=jnp.int32)
    onehot = (assigned[:, None] == expert_ids[None, :]).astype(jnp.int32)
    slot_rank = jnp.sum((jnp.cumsum(onehot, axis=0) - 1) * onehot, axis=1)
    return assigned * capacity + slot_rank


def per_device(
    pair_raw,
    value_raw,
    gate_raw,
    write_strength,
    log_decay,
    segment_ids,
    pair_filter,
    value_filter,
    norm_gain,
    out_weight,
    residual,
    post_gain,
    routes,
    route_weights,
    expert_up,
    expert_down,
):
    partial = mixer(
        pair_raw, value_raw, gate_raw, write_strength, log_decay, segment_ids,
        pair_filter, value_filter, norm_gain, out_weight,
    )
    half = partial.shape[0] // 2
    core = lax.axis_index("head")
    mine = lax.dynamic_slice_in_dim(partial, core * half, half)
    theirs = lax.dynamic_slice_in_dim(partial, (1 - core) * half, half).astype(jnp.bfloat16)
    attention = mine + lax.ppermute(theirs, "head", [(0, 1), (1, 0)]).astype(jnp.float32)
    hidden = (residual.astype(jnp.float32) + attention).astype(jnp.bfloat16)
    expert_in = post_norm(hidden, post_gain)
    devices_all = lax.axis_size("ctx") * lax.axis_size("head")
    local_experts = expert_up.shape[0]
    experts_all = devices_all * local_experts
    local_rows = routes.shape[0]
    top_count = routes.shape[1]
    capacity = local_rows * top_count * 5 // (4 * experts_all)
    slot_index = route_slots(routes, experts_all, capacity)
    owners = jnp.arange(local_rows * top_count, dtype=jnp.int32) // top_count + 1
    owner_table = jnp.zeros((experts_all * capacity,), jnp.int32).at[slot_index].set(owners)
    filled = owner_table > 0
    outgoing = jnp.where(
        filled[:, None], expert_in[jnp.maximum(owner_table - 1, 0)], jnp.zeros((), jnp.bfloat16)
    )
    outgoing = outgoing.reshape(devices_all, local_experts, capacity, expert_in.shape[1])
    answered = expert_apply(
        lax.all_to_all(outgoing, ("ctx", "head"), split_axis=0, concat_axis=0, tiled=True),
        expert_up,
        expert_down,
    )
    returned = lax.all_to_all(answered, ("ctx", "head"), split_axis=0, concat_axis=0, tiled=True)
    result_rows = returned.reshape(-1, expert_in.shape[1])
    chosen_slots = slot_index.reshape(local_rows, top_count)
    combined = hidden.astype(jnp.float32)
    for column in range(top_count):
        combined = combined + route_weights[:, column : column + 1] * result_rows[
            chosen_slots[:, column]
        ].astype(jnp.float32)
    return combined.astype(jnp.bfloat16)


def solution(mesh):
    return jax.shard_map(
        per_device,
        mesh=mesh,
        in_specs=(
            P(("group", "ctx"), None, "head"),
            P(("group", "ctx"), "head"),
            P(("group", "ctx"), "head"),
            P(("group", "ctx"), "head"),
            P(("group", "ctx"), "head"),
            P("group"),
            P(None, None, "head"),
            P(None, "head"),
            P(),
            P("head", None),
            P(("group", "ctx", "head"), None),
            P(),
            P(("group", "ctx", "head"), None),
            P(("group", "ctx", "head"), None),
            P(("ctx", "head"), None, None),
            P(("ctx", "head"), None, None),
        ),
        out_specs=P(("group", "ctx", "head"), None),
        check_vma=False,
    )
```

```python
import functools

import jax
import jax.numpy as jnp
from jax import lax
from jax.experimental import pallas as pl
from jax.experimental.pallas import tpu as pltpu
from jax.sharding import PartitionSpec as P

DK = 128
DV = 128
PAD = 16
EPS = 1e-06
NN = (((1,), (0,)), ((), ()))
NT = (((1,), (1,)), ((), ()))
TN = (((0,), (0,)), ((), ()))
VMEM_MOST = 56 * 1024 * 1024


def dot16(left, right, dims=NN):
    return lax.dot_general(
        left.astype(jnp.bfloat16),
        right.astype(jnp.bfloat16),
        dims,
        preferred_element_type=jnp.float32,
    )


def halves(x):
    high = x.astype(jnp.bfloat16)
    return high, (x - high.astype(jnp.float32)).astype(jnp.bfloat16)


def dot_split(left, right, dims=NN):
    lh, ll = halves(left)
    rh, rl = halves(right)
    return dot16(lh, rh, dims) + (dot16(lh, rl, dims) + dot16(ll, rh, dims))


def silu(x):
    return x * (1.0 / (1.0 + jnp.exp(-x)))


def filtered(raw_ref, taps_ref, match, lanes):
    rows = raw_ref.shape[0] - PAD
    source = raw_ref[:, lanes].astype(jnp.float32)
    taps = taps_ref[:, lanes]
    total = taps[0:1] * source[PAD:]
    for lag in range(1, taps_ref.shape[0]):
        total = total + taps[lag : lag + 1] * (source[PAD - lag : PAD - lag + rows] * match[lag])
    return silu(total)


def unit_rows(x):
    return x * lax.rsqrt(jnp.sum(x * x, axis=-1, keepdims=True) + EPS)


def inverse_unit_lower(coupling, row, col):
    size = coupling.shape[0]
    apart = row ^ col
    inverse = jnp.where(row == col, 1.0, 0.0) - jnp.where(apart == 1, coupling, 0.0)
    step = 2
    while step < size:
        cross = jnp.where((apart >= step) & (apart < 2 * step), coupling, 0.0)
        inverse = inverse - dot16(inverse, dot16(cross, inverse))
        step *= 2
    return inverse


def local_kernel(
    q_ref, k_ref, v_ref, qt_ref, kt_ref, vt_ref, seg_ref, segrow_ref,
    cum_ref, cumrow_ref, beta_ref, qeff_ref, off_ref, maps_ref,
):
    rows = qeff_ref.shape[1]
    seg = seg_ref[...]
    match = [None] + [(seg[:, lag : lag + 1] == seg[:, 0:1]).astype(jnp.float32) for lag in range(1, 4)]
    ids = seg[:, 0:1]
    carried = (ids == seg_ref[0:1, 1:2]).astype(jnp.float32)
    at_end = (ids == seg_ref[rows - 1 : rows, 0:1]).astype(jnp.float32)
    row = lax.broadcasted_iota(jnp.int32, (rows, rows), 0)
    col = lax.broadcasted_iota(jnp.int32, (rows, rows), 1)
    same = ids == segrow_ref[...]
    causal = (row >= col) & same
    strictly = (row > col) & same
    queries = unit_rows(filtered(q_ref, qt_ref, match, slice(None))) * DK ** (-0.5)
    keys = unit_rows(filtered(k_ref, kt_ref, match, slice(None)))
    q16 = queries.astype(jnp.bfloat16)
    k16 = keys.astype(jnp.bfloat16)
    gram = dot16(k16, k16, NT)
    cross = dot16(q16, k16, NT)
    k32 = k16.astype(jnp.float32)
    q32 = q16.astype(jnp.float32)
    eye = (
        lax.broadcasted_iota(jnp.int32, (DK, DK), 0) == lax.broadcasted_iota(jnp.int32, (DK, DK), 1)
    ).astype(jnp.float32)
    for member in range(qeff_ref.shape[0]):
        lanes = slice(member * DV, (member + 1) * DV)
        values = filtered(v_ref, vt_ref, match, lanes)
        cum = cum_ref[member]
        beta = beta_ref[member]
        decay = jnp.exp(jnp.where(causal, cum - cumrow_ref[member], 0.0))
        coupling = jnp.where(strictly, gram * decay * beta, 0.0)
        within = jnp.where(causal, cross * decay, 0.0)
        grown = jnp.exp(cum) * carried
        inverse = inverse_unit_lower(coupling, row, col)
        stacked = jnp.concatenate([values * beta, k32 * (beta * grown)], axis=1)
        solved = dot16(inverse, stacked)
        both = dot16(within, solved)
        off_ref[member] = both[:, :DV]
        qeff_ref[member] = (q32 * grown - both[:, DV:]).astype(jnp.bfloat16)
        final = cum[rows - 1 : rows]
        weighted = k32 * (at_end * jnp.exp(final - cum))
        sums = dot16(solved, weighted, TN)
        shift_t = sums[:DV]
        forward = (jnp.exp(final) * carried[rows - 1 : rows]) * eye - sums[DV:].T
        for half in range(2):
            at = member * 2 + half
            maps_ref[at, :DK, :] = forward.astype(jnp.bfloat16)
            maps_ref[at, DK:, :] = shift_t[half * (DV // 2) : (half + 1) * (DV // 2)].astype(jnp.bfloat16)


def local_maps(pair, value, pair_taps, value_taps, seg, segrow, cum, cumrow, beta):
    heads, rows = beta.shape[:2]
    key_heads = pair.shape[1] // (2 * DK)
    per = heads // key_heads
    padded = pair.shape[0]
    taps = pair_taps.shape[0]
    whole = lambda g: (0, 0)
    return pl.pallas_call(
        local_kernel,
        grid=(key_heads,),
        in_specs=[
            pl.BlockSpec((padded, DK), lambda g: (0, g)),
            pl.BlockSpec((padded, DK), lambda g: (0, key_heads + g)),
            pl.BlockSpec((padded, per * DV), lambda g: (0, g)),
            pl.BlockSpec((taps, DK), lambda g: (0, g)),
            pl.BlockSpec((taps, DK), lambda g: (0, key_heads + g)),
            pl.BlockSpec((taps, per * DV), lambda g: (0, g)),
            pl.BlockSpec((rows, taps), whole),
            pl.BlockSpec((1, rows), whole),
            pl.BlockSpec((per, rows, 1), lambda g: (g, 0, 0)),
            pl.BlockSpec((per, 1, rows), lambda g: (g, 0, 0)),
            pl.BlockSpec((per, rows, 1), lambda g: (g, 0, 0)),
        ],
        out_specs=[
            pl.BlockSpec((per, rows, DK), lambda g: (g, 0, 0)),
            pl.BlockSpec((per, rows, DV), lambda g: (g, 0, 0)),
            pl.BlockSpec((2 * per, DK + DV // 2, DK), lambda g: (g, 0, 0)),
        ],
        out_shape=[
            jax.ShapeDtypeStruct((heads, rows, DK), jnp.bfloat16),
            jax.ShapeDtypeStruct((heads, rows, DV), jnp.float32),
            jax.ShapeDtypeStruct((2 * heads, DK + DV // 2, DK), jnp.bfloat16),
        ],
        compiler_params=pltpu.CompilerParams(vmem_limit_bytes=VMEM_MOST),
        name="local_maps",
    )(pair, pair, value, pair_taps, pair_taps, value_taps, seg, segrow, cum, cumrow, beta)


def carry_kernel(maps_ref, states_ref):
    state = jnp.zeros(states_ref.shape[1:], jnp.float32)
    for at in range(maps_ref.shape[0]):
        states_ref[at] = state.astype(jnp.bfloat16)
        if at + 1 < maps_ref.shape[0]:
            moved = dot16(state, maps_ref[at, :DK, :], NT)
            state = moved + maps_ref[at, DK:, :].astype(jnp.float32)


def carried_states(maps):
    peers = maps.shape[0]
    return pl.pallas_call(
        carry_kernel,
        out_shape=jax.ShapeDtypeStruct((peers, DV // 2, DK), jnp.bfloat16),
        compiler_params=pltpu.CompilerParams(vmem_limit_bytes=VMEM_MOST),
        name="carried_states",
    )(maps)


def emit_kernel(qeff_ref, off_ref, state_ref, gate_ref, gain_ref, weight_ref, out_ref, gated_ref):
    heads = qeff_ref.shape[0]
    gain = gain_ref[...]
    for head in range(heads):
        lanes = slice(head * DV, (head + 1) * DV)
        mixed = off_ref[head] + dot16(qeff_ref[head], state_ref[head], NT)
        scale = lax.rsqrt(jnp.mean(mixed * mixed, axis=-1, keepdims=True) + EPS)
        gate = silu(gate_ref[:, lanes].astype(jnp.float32))
        gated_ref[:, lanes] = (mixed * scale * gain * gate).astype(jnp.bfloat16)
    width = out_ref.shape[1]
    tile = 512
    for at in range(0, width, tile):
        out_ref[:, at : at + tile] = jnp.dot(
            gated_ref[...], weight_ref[:, at : at + tile], preferred_element_type=jnp.float32
        )


def emitted_rows(qeff, off, states, gate_raw, gain, weight):
    rows, channels = gate_raw.shape
    return pl.pallas_call(
        emit_kernel,
        out_shape=jax.ShapeDtypeStruct((rows, weight.shape[1]), jnp.float32),
        scratch_shapes=[pltpu.VMEM((rows, channels), jnp.bfloat16)],
        compiler_params=pltpu.CompilerParams(vmem_limit_bytes=VMEM_MOST),
        name="emitted_rows",
    )(qeff, off, states, gate_raw, gain, weight)


def mixer(
    pair_raw, value_raw, gate_raw, write_strength, log_decay, segment_ids,
    pair_filter, value_filter, norm_gain, out_weight,
):
    rows = pair_raw.shape[0]
    taps = value_filter.shape[0]
    peers = lax.axis_size("ctx")
    pair = pair_raw.reshape(rows, -1)
    width = pair.shape[1]
    rim = jnp.concatenate([pair[rows - PAD :], value_raw[rows - PAD :]], axis=1)
    before = lax.ppermute(rim, "ctx", [(i, i + 1) for i in range(peers - 1)])
    first = lax.axis_index("ctx") * rows
    padded_ids = jnp.concatenate([jnp.full((taps - 1,), -1, jnp.int32), segment_ids])
    ids = lax.dynamic_slice_in_dim(padded_ids, first, rows + taps - 1)
    seg = jnp.stack([ids[taps - 1 - lag : taps - 1 - lag + rows] for lag in range(taps)], axis=1)
    segrow = ids[taps - 1 :][None, :]
    cum = jnp.cumsum(log_decay, axis=0).T
    qeff, off, maps = local_maps(
        jnp.concatenate([before[:, :width], pair]),
        jnp.concatenate([before[:, width:], value_raw]),
        pair_filter.reshape(taps, -1),
        value_filter,
        seg,
        segrow,
        cum[:, :, None],
        cum[:, None, :],
        write_strength.T[:, :, None],
    )
    heads = qeff.shape[0]
    arrived = lax.all_to_all(maps, "ctx", split_axis=0, concat_axis=0, tiled=True)
    states = lax.all_to_all(carried_states(arrived), "ctx", split_axis=0, concat_axis=0, tiled=True)
    states = states.reshape(heads, DV, DK)
    return emitted_rows(qeff, off, states, gate_raw, norm_gain[None, :], out_weight)

PLANE = 4
AGZ, AGX, AGY, AGA, AGB, DA, DB, XA, XB, YA, YB, RSZ = range(12)


def expert_kernel(
    x_ref, slot_ref, weight_ref, up_mine, up_other, down_mine, down_other, out_ref,
    got, part, diag, from_x, from_y, sums, from_z, up, down, rows_in, rows_out, chosen,
    send_sem, recv_sem, local_sem,
):
    planes = got.shape[0] // PLANE
    tokens = got.shape[1]
    half = tokens // 2
    first, second = pl.ds(0, half), pl.ds(half, half)
    slots = rows_in.shape[0]
    me = lax.axis_index("ctx")
    x, y, z = me % 2, (me // 2) % 2, me // PLANE
    beside_x = me + 1 - 2 * x
    beside_y = me + 2 - 4 * y

    def plane_of(k):
        return (z % 2 + k % 2) % 2 + 2 * ((z // 2 + k // 2) % 2)

    def along_z(k):
        return PLANE * plane_of(k) + 2 * y + x

    def block(k, flip_y, flip_x):
        row = 1 - y if flip_y else y
        column = 1 - x if flip_x else x
        return PLANE * plane_of(k) + 2 * row + column

    def copy(kind, k, source, target, device):
        return pltpu.make_async_remote_copy(
            src_ref=source,
            dst_ref=target,
            send_sem=send_sem.at[kind, k],
            recv_sem=recv_sem.at[kind, k],
            device_id={"ctx": device},
            device_id_type=pl.DeviceIdType.MESH,
        )

    def arrived(kind, k, place, device):
        copy(kind, k, place, place, device).wait_recv()

    loads = [
        pltpu.make_async_copy(source, target, local_sem.at[at])
        for at, (source, target) in enumerate(
            [
                (up_mine.at[0], up.at[0]),
                (up_other.at[0], up.at[1]),
                (down_mine.at[0], down.at[0]),
                (down_other.at[0], down.at[1]),
            ]
        )
    ]
    for load in loads:
        load.start()
    got[me] = x_ref[...]

    partners = [beside_x, beside_y] + [along_z(k) for k in range(1, planes)]
    barrier = pltpu.get_barrier_semaphore()
    for partner in partners:
        pl.semaphore_signal(
            barrier, inc=1, device_id={"ctx": partner}, device_id_type=pl.DeviceIdType.MESH
        )
    pl.semaphore_wait(barrier, len(partners))

    def share_in_plane(k):
        own = block(k, False, False)
        copy(AGX, k, got.at[own], got.at[own], beside_x).start()
        copy(AGY, k, got.at[own], got.at[own], beside_y).start()

    share_in_plane(0)
    for k in range(1, planes):
        copy(AGZ, k, got.at[me], got.at[me], along_z(k)).start()
    for load in loads:
        load.wait()

    def experts(k):
        plane = plane_of(k)
        base = PLANE * plane
        slot_rows = slot_ref[plane]
        weight_rows = weight_ref[plane]
        place = lax.broadcasted_iota(jnp.int32, (slots, PLANE * tokens), 0)
        source = got[pl.ds(base, PLANE)].reshape(PLANE * tokens, got.shape[2])
        for e in range(2):
            here = place == slot_rows[e : e + 1]
            pick = jnp.where(here, 1.0, 0.0).astype(jnp.bfloat16)
            chosen[pl.ds(e * slots, slots), :] = jnp.where(here, weight_rows[e : e + 1], 0.0).astype(
                jnp.bfloat16
            )
            rows_in[...] = jnp.dot(pick, source, preferred_element_type=jnp.float32).astype(
                jnp.bfloat16
            )
            units = jnp.dot(rows_in[...], up[e], preferred_element_type=jnp.float32)
            width = units.shape[1] // 2
            active = (silu(units[:, :width]) * units[:, width:]).astype(jnp.bfloat16)
            rows_out[pl.ds(e * slots, slots), :] = jnp.dot(
                active, down[e], preferred_element_type=jnp.float32
            ).astype(jnp.bfloat16)
        for b in range(PLANE):
            part[base + b] = lax.dot_general(
                chosen[:, b * tokens : (b + 1) * tokens],
                rows_out[...],
                TN,
                preferred_element_type=jnp.float32,
            ).astype(jnp.bfloat16)

    def give_first(k):
        across, xb, yb = block(k, True, True), block(k, False, True), block(k, True, False)
        copy(DA, k, part.at[across, first], diag.at[k, first], beside_y).start()
        copy(DB, k, part.at[across, second], diag.at[k, second], beside_x).start()
        copy(XB, k, part.at[xb, second], from_x.at[k, second], beside_x).start()
        copy(YA, k, part.at[yb, first], from_y.at[k, first], beside_y).start()

    def give_second(k):
        xb, yb = block(k, False, True), block(k, True, False)
        arrived(DA, k, diag.at[k, first], beside_y)
        part[xb, first] = (
            part[xb, first].astype(jnp.float32) + diag[k, first].astype(jnp.float32)
        ).astype(jnp.bfloat16)
        copy(XA, k, part.at[xb, first], from_x.at[k, first], beside_x).start()
        arrived(DB, k, diag.at[k, second], beside_x)
        part[yb, second] = (
            part[yb, second].astype(jnp.float32) + diag[k, second].astype(jnp.float32)
        ).astype(jnp.bfloat16)
        copy(YB, k, part.at[yb, second], from_y.at[k, second], beside_y).start()

    def plane_sum(k):
        arrived(XA, k, from_x.at[k, first], beside_x)
        arrived(XB, k, from_x.at[k, second], beside_x)
        arrived(YA, k, from_y.at[k, first], beside_y)
        arrived(YB, k, from_y.at[k, second], beside_y)
        own = block(k, False, False)
        return (
            part[own].astype(jnp.float32)
            + from_x[k].astype(jnp.float32)
            + from_y[k].astype(jnp.float32)
        )

    def give_third(k):
        sums[k] = plane_sum(k).astype(jnp.bfloat16)
        copy(RSZ, k, sums.at[k], from_z.at[k], along_z(k)).start()

    def turn(k, unused):
        across_x, across_y = block(k, False, True), block(k, True, False)
        arrived(AGX, k, got.at[across_x], beside_x)
        copy(AGA, k, got.at[across_x, first], got.at[across_x, first], beside_y).start()
        arrived(AGY, k, got.at[across_y], beside_y)
        copy(AGB, k, got.at[across_y, second], got.at[across_y, second], beside_x).start()

        @pl.when(k < planes - 1)
        def _():
            arrived(AGZ, k + 1, got.at[along_z(k + 1)], along_z(k + 1))
            share_in_plane(k + 1)

        across = block(k, True, True)
        arrived(AGA, k, got.at[across, first], beside_y)
        arrived(AGB, k, got.at[across, second], beside_x)
        experts(k)

        @pl.when(k >= 1)
        def _():
            give_first(k)

        @pl.when(k >= 2)
        def _():
            give_second(k - 1)

        @pl.when(k >= 3)
        def _():
            give_third(k - 2)

        return unused

    lax.fori_loop(0, planes, turn, 0)
    give_first(0)
    give_second(3)
    give_third(2)
    give_second(0)
    give_third(3)
    total = plane_sum(0)
    for k in range(1, planes):
        arrived(RSZ, k, from_z.at[k], along_z(k))
        total = total + from_z[k].astype(jnp.float32)
    out_ref[...] = total

    for k in range(planes):
        for kind in (AGX, AGY):
            copy(kind, k, got.at[0], got.at[0], beside_x).wait_send()
        for kind in (AGA, AGB):
            copy(kind, k, got.at[0, first], got.at[0, first], beside_x).wait_send()
        for kind in (DA, DB, XA, XB, YA, YB):
            copy(kind, k, part.at[0, first], diag.at[0, first], beside_x).wait_send()
        if k > 0:
            copy(AGZ, k, got.at[0], got.at[0], beside_x).wait_send()
            copy(RSZ, k, sums.at[0], from_z.at[0], beside_x).wait_send()


def expert_sums(x, slot, weight, up_mine, up_other, down_mine, down_other, capacity):
    peers = lax.axis_size("ctx")
    planes = peers // PLANE
    assert planes == 4 and x.shape[0] % 32 == 0
    tokens, width = x.shape
    units = up_mine.shape[2]
    slots = (PLANE * capacity + 15) // 16 * 16
    vmem = pl.BlockSpec(memory_space=pltpu.VMEM)
    hbm = pl.BlockSpec(memory_space=pl.ANY)
    half = jnp.bfloat16
    return pl.pallas_call(
        expert_kernel,
        out_shape=jax.ShapeDtypeStruct((tokens, width), jnp.float32),
        in_specs=[vmem, vmem, vmem, hbm, hbm, hbm, hbm],
        out_specs=vmem,
        scratch_shapes=[
            pltpu.VMEM((peers, tokens, width), half),
            pltpu.VMEM((peers, tokens, width), half),
            pltpu.VMEM((planes, tokens, width), half),
            pltpu.VMEM((planes, tokens, width), half),
            pltpu.VMEM((planes, tokens, width), half),
            pltpu.VMEM((planes, tokens, width), half),
            pltpu.VMEM((planes, tokens, width), half),
            pltpu.VMEM((2, width, units), half),
            pltpu.VMEM((2, units // 2, width), half),
            pltpu.VMEM((slots, width), half),
            pltpu.VMEM((2 * slots, width), half),
            pltpu.VMEM((2 * slots, PLANE * tokens), half),
            pltpu.SemaphoreType.DMA((12, planes)),
            pltpu.SemaphoreType.DMA((12, planes)),
            pltpu.SemaphoreType.DMA((4,)),
        ],
        compiler_params=pltpu.CompilerParams(
            collective_id=0, has_side_effects=True, vmem_limit_bytes=VMEM_MOST
        ),
        name="expert_sums",
    )(x, slot, weight, up_mine, up_other, down_mine, down_other)


def route_tables(routes, route_weights):
    peers, cores = lax.axis_size("ctx"), lax.axis_size("head")
    experts = jnp.arange(peers * cores, dtype=jnp.int32)
    named = (routes[None] == experts[:, None, None]).astype(jnp.float32)
    dense = jnp.sum(named * route_weights[None], axis=2)
    tokens = routes.shape[0]
    seen = lax.all_to_all(
        dense.reshape(peers, cores, tokens), "ctx", split_axis=0, concat_axis=0, tiled=True
    )
    seen = jnp.where(lax.axis_index("head") == 0, seen, seen[:, ::-1])
    seen = seen.reshape(peers // PLANE, PLANE, cores, tokens).swapaxes(1, 2)
    seen = seen.reshape(peers // PLANE, cores, PLANE * tokens)
    filled = seen > 0
    span = PLANE * tokens
    upto = (
        lax.broadcasted_iota(jnp.int32, (span, span), 0)
        <= lax.broadcasted_iota(jnp.int32, (span, span), 1)
    ).astype(jnp.bfloat16)
    rank = jnp.dot(
        filled.reshape(-1, span).astype(jnp.bfloat16), upto, preferred_element_type=jnp.float32
    ).reshape(seen.shape)
    return jnp.where(filled, rank.astype(jnp.int32) - 1, -1), seen


def post_norm(hidden, post_gain):
    hidden_full = hidden.astype(jnp.float32)
    square_mean = jnp.mean(hidden_full * hidden_full, axis=-1, keepdims=True)
    return (hidden_full / jnp.sqrt(square_mean + 1e-06) * post_gain).astype(jnp.bfloat16)


def per_device(
    pair_raw,
    value_raw,
    gate_raw,
    write_strength,
    log_decay,
    segment_ids,
    pair_filter,
    value_filter,
    norm_gain,
    out_weight,
    residual,
    post_gain,
    routes,
    route_weights,
    expert_up,
    expert_down,
):
    swap = [(0, 1), (1, 0)]
    devices_all = lax.axis_size("ctx") * lax.axis_size("head")
    up_other = lax.ppermute(expert_up, "head", swap)
    down_other = lax.ppermute(expert_down, "head", swap)
    slot, weight = route_tables(routes, route_weights)
    partial = mixer(
        pair_raw, value_raw, gate_raw, write_strength, log_decay, segment_ids,
        pair_filter, value_filter, norm_gain, out_weight,
    )
    half = partial.shape[0] // 2
    core = lax.axis_index("head")
    mine = lax.dynamic_slice_in_dim(partial, core * half, half)
    theirs = lax.dynamic_slice_in_dim(partial, (1 - core) * half, half).astype(jnp.bfloat16)
    attention = mine + lax.ppermute(theirs, "head", swap).astype(jnp.float32)
    hidden = (residual.astype(jnp.float32) + attention).astype(jnp.bfloat16)
    expert_in = post_norm(hidden, post_gain)
    capacity = routes.shape[0] * routes.shape[1] * 5 // (4 * devices_all)
    answered = expert_sums(
        expert_in, slot, weight, expert_up, up_other, expert_down, down_other, capacity
    )
    return (hidden.astype(jnp.float32) + answered).astype(jnp.bfloat16)


def solution(mesh):
    return jax.shard_map(
        per_device,
        mesh=mesh,
        in_specs=(
            P(("group", "ctx"), None, "head"),
            P(("group", "ctx"), "head"),
            P(("group", "ctx"), "head"),
            P(("group", "ctx"), "head"),
            P(("group", "ctx"), "head"),
            P("group"),
            P(None, None, "head"),
            P(None, "head"),
            P(),
            P("head", None),
            P(("group", "ctx", "head"), None),
            P(),
            P(("group", "ctx", "head"), None),
            P(("group", "ctx", "head"), None),
            P(("ctx", "head"), None, None),
            P(("ctx", "head"), None, None),
        ),
        out_specs=P(("group", "ctx", "head"), None),
        check_vma=False,
    )
```

```python
import functools

import jax
import jax.numpy as jnp
from jax import lax
from jax.experimental import pallas as pl
from jax.experimental.pallas import tpu as pltpu
from jax.sharding import PartitionSpec as P

DK = 128
DV = 128
PAD = 16
EPS = 1e-06
NN = (((1,), (0,)), ((), ()))
NT = (((1,), (1,)), ((), ()))
TN = (((0,), (0,)), ((), ()))
VMEM_MOST = 56 * 1024 * 1024


def dot16(left, right, dims=NN):
    return lax.dot_general(
        left.astype(jnp.bfloat16),
        right.astype(jnp.bfloat16),
        dims,
        preferred_element_type=jnp.float32,
    )


def halves(x):
    high = x.astype(jnp.bfloat16)
    return high, (x - high.astype(jnp.float32)).astype(jnp.bfloat16)


def dot_split(left, right, dims=NN):
    lh, ll = halves(left)
    rh, rl = halves(right)
    return dot16(lh, rh, dims) + (dot16(lh, rl, dims) + dot16(ll, rh, dims))


def silu(x):
    return x * (1.0 / (1.0 + jnp.exp(-x)))


def filtered(raw_ref, taps_ref, match, lanes):
    rows = raw_ref.shape[0] - PAD
    source = raw_ref[:, lanes].astype(jnp.float32)
    taps = taps_ref[:, lanes]
    total = taps[0:1] * source[PAD:]
    for lag in range(1, taps_ref.shape[0]):
        total = total + taps[lag : lag + 1] * (source[PAD - lag : PAD - lag + rows] * match[lag])
    return silu(total)


def unit_rows(x):
    return x * lax.rsqrt(jnp.sum(x * x, axis=-1, keepdims=True) + EPS)


def inverse_unit_lower(coupling, row, col):
    size = coupling.shape[0]
    apart = row ^ col
    inverse = jnp.where(row == col, 1.0, 0.0) - jnp.where(apart == 1, coupling, 0.0)
    step = 2
    while step < size:
        cross = jnp.where((apart >= step) & (apart < 2 * step), coupling, 0.0)
        inverse = inverse - dot16(inverse, dot16(cross, inverse))
        step *= 2
    return inverse


def local_kernel(
    q_ref, k_ref, v_ref, qt_ref, kt_ref, vt_ref, seg_ref, segrow_ref,
    cum_ref, cumrow_ref, beta_ref, table_ref, qeff_ref, off_ref, maps_ref,
):
    rows = qeff_ref.shape[1]
    maps_ref[:, DK + DV // 2 :, :] = table_ref[...]
    seg = seg_ref[...]
    match = [None] + [(seg[:, lag : lag + 1] == seg[:, 0:1]).astype(jnp.float32) for lag in range(1, 4)]
    ids = seg[:, 0:1]
    carried = (ids == seg_ref[0:1, 1:2]).astype(jnp.float32)
    at_end = (ids == seg_ref[rows - 1 : rows, 0:1]).astype(jnp.float32)
    row = lax.broadcasted_iota(jnp.int32, (rows, rows), 0)
    col = lax.broadcasted_iota(jnp.int32, (rows, rows), 1)
    same = ids == segrow_ref[...]
    causal = (row >= col) & same
    strictly = (row > col) & same
    queries = unit_rows(filtered(q_ref, qt_ref, match, slice(None))) * DK ** (-0.5)
    keys = unit_rows(filtered(k_ref, kt_ref, match, slice(None)))
    q16 = queries.astype(jnp.bfloat16)
    k16 = keys.astype(jnp.bfloat16)
    gram = dot16(k16, k16, NT)
    cross = dot16(q16, k16, NT)
    k32 = k16.astype(jnp.float32)
    q32 = q16.astype(jnp.float32)
    eye = (
        lax.broadcasted_iota(jnp.int32, (DK, DK), 0) == lax.broadcasted_iota(jnp.int32, (DK, DK), 1)
    ).astype(jnp.float32)
    for member in range(qeff_ref.shape[0]):
        lanes = slice(member * DV, (member + 1) * DV)
        values = filtered(v_ref, vt_ref, match, lanes)
        cum = cum_ref[member]
        beta = beta_ref[member]
        decay = jnp.exp(jnp.where(causal, cum - cumrow_ref[member], 0.0))
        coupling = jnp.where(strictly, gram * decay * beta, 0.0)
        within = jnp.where(causal, cross * decay, 0.0)
        grown = jnp.exp(cum) * carried
        inverse = inverse_unit_lower(coupling, row, col)
        stacked = jnp.concatenate([values * beta, k32 * (beta * grown)], axis=1)
        solved = dot16(inverse, stacked)
        both = dot16(within, solved)
        off_ref[member] = both[:, :DV]
        qeff_ref[member] = (q32 * grown - both[:, DV:]).astype(jnp.bfloat16)
        final = cum[rows - 1 : rows]
        weighted = k32 * (at_end * jnp.exp(final - cum))
        sums = dot16(solved, weighted, TN)
        shift_t = sums[:DV]
        forward = (jnp.exp(final) * carried[rows - 1 : rows]) * eye - sums[DV:].T
        for half in range(2):
            at = member * 2 + half
            maps_ref[at, :DK, :] = forward.astype(jnp.bfloat16)
            maps_ref[at, DK : DK + DV // 2, :] = shift_t[half * (DV // 2) : (half + 1) * (DV // 2)].astype(jnp.bfloat16)


def local_maps(pair, value, pair_taps, value_taps, seg, segrow, cum, cumrow, beta, table):
    heads, rows = beta.shape[:2]
    key_heads = pair.shape[1] // (2 * DK)
    per = heads // key_heads
    extra = table.shape[1]
    padded = pair.shape[0]
    taps = pair_taps.shape[0]
    whole = lambda g: (0, 0)
    return pl.pallas_call(
        local_kernel,
        grid=(key_heads,),
        in_specs=[
            pl.BlockSpec((padded, DK), lambda g: (0, g)),
            pl.BlockSpec((padded, DK), lambda g: (0, key_heads + g)),
            pl.BlockSpec((padded, per * DV), lambda g: (0, g)),
            pl.BlockSpec((taps, DK), lambda g: (0, g)),
            pl.BlockSpec((taps, DK), lambda g: (0, key_heads + g)),
            pl.BlockSpec((taps, per * DV), lambda g: (0, g)),
            pl.BlockSpec((rows, taps), whole),
            pl.BlockSpec((1, rows), whole),
            pl.BlockSpec((per, rows, 1), lambda g: (g, 0, 0)),
            pl.BlockSpec((per, 1, rows), lambda g: (g, 0, 0)),
            pl.BlockSpec((per, rows, 1), lambda g: (g, 0, 0)),
            pl.BlockSpec((2 * per, extra, DK), lambda g: (g, 0, 0)),
        ],
        out_specs=[
            pl.BlockSpec((per, rows, DK), lambda g: (g, 0, 0)),
            pl.BlockSpec((per, rows, DV), lambda g: (g, 0, 0)),
            pl.BlockSpec((2 * per, DK + DV // 2 + extra, DK), lambda g: (g, 0, 0)),
        ],
        out_shape=[
            jax.ShapeDtypeStruct((heads, rows, DK), jnp.bfloat16),
            jax.ShapeDtypeStruct((heads, rows, DV), jnp.float32),
            jax.ShapeDtypeStruct((2 * heads, DK + DV // 2 + extra, DK), jnp.bfloat16),
        ],
        compiler_params=pltpu.CompilerParams(vmem_limit_bytes=VMEM_MOST),
        name="local_maps",
    )(pair, pair, value, pair_taps, pair_taps, value_taps, seg, segrow, cum, cumrow, beta, table)


def carry_kernel(maps_ref, states_ref):
    state = jnp.zeros(states_ref.shape[1:], jnp.float32)
    for at in range(maps_ref.shape[0]):
        states_ref[at] = state.astype(jnp.bfloat16)
        if at + 1 < maps_ref.shape[0]:
            moved = dot16(state, maps_ref[at, :DK, :], NT)
            state = moved + maps_ref[at, DK : DK + DV // 2, :].astype(jnp.float32)


def carried_states(maps):
    peers = maps.shape[0]
    return pl.pallas_call(
        carry_kernel,
        out_shape=jax.ShapeDtypeStruct((peers, DV // 2, DK), jnp.bfloat16),
        compiler_params=pltpu.CompilerParams(vmem_limit_bytes=VMEM_MOST),
        name="carried_states",
    )(maps)


def emit_kernel(qeff_ref, off_ref, state_ref, gate_ref, gain_ref, weight_ref, out_ref, gated_ref):
    heads = qeff_ref.shape[0]
    gain = gain_ref[...]
    for head in range(heads):
        lanes = slice(head * DV, (head + 1) * DV)
        mixed = off_ref[head] + dot16(qeff_ref[head], state_ref[head], NT)
        scale = lax.rsqrt(jnp.mean(mixed * mixed, axis=-1, keepdims=True) + EPS)
        gate = silu(gate_ref[:, lanes].astype(jnp.float32))
        gated_ref[:, lanes] = (mixed * scale * gain * gate).astype(jnp.bfloat16)
    width = out_ref.shape[1]
    tile = 512
    for at in range(0, width, tile):
        out_ref[:, at : at + tile] = jnp.dot(
            gated_ref[...], weight_ref[:, at : at + tile], preferred_element_type=jnp.float32
        )


def emitted_rows(qeff, off, states, gate_raw, gain, weight):
    rows, channels = gate_raw.shape
    return pl.pallas_call(
        emit_kernel,
        out_shape=jax.ShapeDtypeStruct((rows, weight.shape[1]), jnp.float32),
        scratch_shapes=[pltpu.VMEM((rows, channels), jnp.bfloat16)],
        compiler_params=pltpu.CompilerParams(vmem_limit_bytes=VMEM_MOST),
        name="emitted_rows",
    )(qeff, off, states, gate_raw, gain, weight)


def mixer(
    pair_raw, value_raw, gate_raw, write_strength, log_decay, segment_ids,
    pair_filter, value_filter, norm_gain, out_weight, table,
):
    rows = pair_raw.shape[0]
    taps = value_filter.shape[0]
    peers = lax.axis_size("ctx")
    pair = pair_raw.reshape(rows, -1)
    width = pair.shape[1]
    rim = jnp.concatenate([pair[rows - PAD :], value_raw[rows - PAD :]], axis=1)
    before = lax.ppermute(rim, "ctx", [(i, i + 1) for i in range(peers - 1)])
    first = lax.axis_index("ctx") * rows
    padded_ids = jnp.concatenate([jnp.full((taps - 1,), -1, jnp.int32), segment_ids])
    ids = lax.dynamic_slice_in_dim(padded_ids, first, rows + taps - 1)
    seg = jnp.stack([ids[taps - 1 - lag : taps - 1 - lag + rows] for lag in range(taps)], axis=1)
    segrow = ids[taps - 1 :][None, :]
    cum = jnp.cumsum(log_decay, axis=0).T
    qeff, off, maps = local_maps(
        jnp.concatenate([before[:, :width], pair]),
        jnp.concatenate([before[:, width:], value_raw]),
        pair_filter.reshape(taps, -1),
        value_filter,
        seg,
        segrow,
        cum[:, :, None],
        cum[:, None, :],
        write_strength.T[:, :, None],
        table,
    )
    heads = qeff.shape[0]
    arrived = lax.all_to_all(maps, "ctx", split_axis=0, concat_axis=0, tiled=True)
    states = lax.all_to_all(carried_states(arrived), "ctx", split_axis=0, concat_axis=0, tiled=True)
    states = states.reshape(heads, DV, DK)
    partial = emitted_rows(qeff, off, states, gate_raw, norm_gain[None, :], out_weight)
    return partial, arrived[:, DK + DV // 2 :]

PLANE = 4
AGZ, AGX, AGY, AGA, AGB, DA, DB, XA, XB, YA, YB, RSZ = range(12)


def expert_kernel(
    x_ref, slot_ref, weight_ref, up_mine, up_other, down_mine, down_other, out_ref,
    got, part, diag, from_x, from_y, sums, from_z, up, down, rows_in, rows_out, chosen,
    send_sem, recv_sem, local_sem,
):
    planes = got.shape[0] // PLANE
    tokens = got.shape[1]
    half = tokens // 2
    first, second = pl.ds(0, half), pl.ds(half, half)
    slots = rows_in.shape[0]
    me = lax.axis_index("ctx")
    x, y, z = me % 2, (me // 2) % 2, me // PLANE
    beside_x = me + 1 - 2 * x
    beside_y = me + 2 - 4 * y

    def plane_of(k):
        return (z % 2 + k % 2) % 2 + 2 * ((z // 2 + k // 2) % 2)

    def along_z(k):
        return PLANE * plane_of(k) + 2 * y + x

    def block(k, flip_y, flip_x):
        row = 1 - y if flip_y else y
        column = 1 - x if flip_x else x
        return PLANE * plane_of(k) + 2 * row + column

    def copy(kind, k, source, target, device):
        return pltpu.make_async_remote_copy(
            src_ref=source,
            dst_ref=target,
            send_sem=send_sem.at[kind, k],
            recv_sem=recv_sem.at[kind, k],
            device_id={"ctx": device},
            device_id_type=pl.DeviceIdType.MESH,
        )

    def arrived(kind, k, place, device):
        copy(kind, k, place, place, device).wait_recv()

    loads = [
        pltpu.make_async_copy(source, target, local_sem.at[at])
        for at, (source, target) in enumerate(
            [
                (up_mine.at[0], up.at[0]),
                (up_other.at[0], up.at[1]),
                (down_mine.at[0], down.at[0]),
                (down_other.at[0], down.at[1]),
            ]
        )
    ]
    for load in loads:
        load.start()
    got[me] = x_ref[...]

    partners = [beside_x, beside_y] + [along_z(k) for k in range(1, planes)]
    barrier = pltpu.get_barrier_semaphore()
    for partner in partners:
        pl.semaphore_signal(
            barrier, inc=1, device_id={"ctx": partner}, device_id_type=pl.DeviceIdType.MESH
        )
    pl.semaphore_wait(barrier, len(partners))

    def share_in_plane(k):
        own = block(k, False, False)
        copy(AGX, k, got.at[own], got.at[own], beside_x).start()
        copy(AGY, k, got.at[own], got.at[own], beside_y).start()

    def share_along_z(k):
        copy(AGZ, k, got.at[me], got.at[me], along_z(k)).start()

    def pass_on(k):
        across_x, across_y = block(k, False, True), block(k, True, False)
        arrived(AGX, k, got.at[across_x], beside_x)
        copy(AGA, k, got.at[across_x, first], got.at[across_x, first], beside_y).start()
        arrived(AGY, k, got.at[across_y], beside_y)
        copy(AGB, k, got.at[across_y, second], got.at[across_y, second], beside_x).start()

    def take_from_z(k):
        arrived(AGZ, k, got.at[along_z(k)], along_z(k))
        share_in_plane(k)

    share_in_plane(0)
    share_along_z(1)
    pass_on(0)
    share_along_z(2)
    take_from_z(1)
    for load in loads:
        load.wait()

    def experts(k):
        plane = plane_of(k)
        base = PLANE * plane
        slot_rows = slot_ref[plane]
        weight_rows = weight_ref[plane]
        place = lax.broadcasted_iota(jnp.int32, (slots, PLANE * tokens), 0)
        source = got[pl.ds(base, PLANE)].reshape(PLANE * tokens, got.shape[2])
        for e in range(2):
            here = place == slot_rows[e : e + 1]
            pick = jnp.where(here, 1.0, 0.0).astype(jnp.bfloat16)
            chosen[pl.ds(e * slots, slots), :] = jnp.where(here, weight_rows[e : e + 1], 0.0).astype(
                jnp.bfloat16
            )
            rows_in[...] = jnp.dot(pick, source, preferred_element_type=jnp.float32).astype(
                jnp.bfloat16
            )
            units = jnp.dot(rows_in[...], up[e], preferred_element_type=jnp.float32)
            width = units.shape[1] // 2
            active = (silu(units[:, :width]) * units[:, width:]).astype(jnp.bfloat16)
            rows_out[pl.ds(e * slots, slots), :] = jnp.dot(
                active, down[e], preferred_element_type=jnp.float32
            ).astype(jnp.bfloat16)
        for b in range(PLANE):
            part[base + b] = lax.dot_general(
                chosen[:, b * tokens : (b + 1) * tokens],
                rows_out[...],
                TN,
                preferred_element_type=jnp.float32,
            ).astype(jnp.bfloat16)

    def give_first(k):
        across, xb, yb = block(k, True, True), block(k, False, True), block(k, True, False)
        copy(DA, k, part.at[across, first], diag.at[k, first], beside_y).start()
        copy(DB, k, part.at[across, second], diag.at[k, second], beside_x).start()
        copy(XB, k, part.at[xb, second], from_x.at[k, second], beside_x).start()
        copy(YA, k, part.at[yb, first], from_y.at[k, first], beside_y).start()

    def give_second(k):
        xb, yb = block(k, False, True), block(k, True, False)
        arrived(DA, k, diag.at[k, first], beside_y)
        part[xb, first] = (
            part[xb, first].astype(jnp.float32) + diag[k, first].astype(jnp.float32)
        ).astype(jnp.bfloat16)
        copy(XA, k, part.at[xb, first], from_x.at[k, first], beside_x).start()
        arrived(DB, k, diag.at[k, second], beside_x)
        part[yb, second] = (
            part[yb, second].astype(jnp.float32) + diag[k, second].astype(jnp.float32)
        ).astype(jnp.bfloat16)
        copy(YB, k, part.at[yb, second], from_y.at[k, second], beside_y).start()

    def plane_sum(k):
        arrived(XA, k, from_x.at[k, first], beside_x)
        arrived(XB, k, from_x.at[k, second], beside_x)
        arrived(YA, k, from_y.at[k, first], beside_y)
        arrived(YB, k, from_y.at[k, second], beside_y)
        own = block(k, False, False)
        return (
            part[own].astype(jnp.float32)
            + from_x[k].astype(jnp.float32)
            + from_y[k].astype(jnp.float32)
        )

    def give_third(k):
        sums[k] = plane_sum(k).astype(jnp.bfloat16)
        copy(RSZ, k, sums.at[k], from_z.at[k], along_z(k)).start()

    def turn(k, unused):
        @pl.when(k < planes - 1)
        def _():
            pass_on(k + 1)

        @pl.when(k == 0)
        def _():
            share_along_z(3)
            take_from_z(2)

        across = block(k, True, True)
        arrived(AGA, k, got.at[across, first], beside_y)
        arrived(AGB, k, got.at[across, second], beside_x)
        experts(k)

        @pl.when(k >= 1)
        def _():
            give_first(k)

        @pl.when(k == 1)
        def _():
            take_from_z(3)

        @pl.when(k >= 2)
        def _():
            give_second(k - 1)

        @pl.when(k >= 3)
        def _():
            give_third(k - 2)

        return unused

    lax.fori_loop(0, planes, turn, 0)
    give_first(0)
    give_second(3)
    give_third(2)
    give_second(0)
    give_third(3)
    total = plane_sum(0)
    for k in range(1, planes):
        arrived(RSZ, k, from_z.at[k], along_z(k))
        total = total + from_z[k].astype(jnp.float32)
    out_ref[...] = total

    for k in range(planes):
        for kind in (AGX, AGY):
            copy(kind, k, got.at[0], got.at[0], beside_x).wait_send()
        for kind in (AGA, AGB):
            copy(kind, k, got.at[0, first], got.at[0, first], beside_x).wait_send()
        for kind in (DA, DB, XA, XB, YA, YB):
            copy(kind, k, part.at[0, first], diag.at[0, first], beside_x).wait_send()
        if k > 0:
            copy(AGZ, k, got.at[0], got.at[0], beside_x).wait_send()
            copy(RSZ, k, sums.at[0], from_z.at[0], beside_x).wait_send()


def expert_sums(x, slot, weight, up_mine, up_other, down_mine, down_other, capacity):
    peers = lax.axis_size("ctx")
    planes = peers // PLANE
    assert planes == 4 and x.shape[0] % 32 == 0
    tokens, width = x.shape
    units = up_mine.shape[2]
    slots = (PLANE * capacity + 15) // 16 * 16
    vmem = pl.BlockSpec(memory_space=pltpu.VMEM)
    hbm = pl.BlockSpec(memory_space=pl.ANY)
    half = jnp.bfloat16
    return pl.pallas_call(
        expert_kernel,
        out_shape=jax.ShapeDtypeStruct((tokens, width), jnp.float32),
        in_specs=[vmem, vmem, vmem, hbm, hbm, hbm, hbm],
        out_specs=vmem,
        scratch_shapes=[
            pltpu.VMEM((peers, tokens, width), half),
            pltpu.VMEM((peers, tokens, width), half),
            pltpu.VMEM((planes, tokens, width), half),
            pltpu.VMEM((planes, tokens, width), half),
            pltpu.VMEM((planes, tokens, width), half),
            pltpu.VMEM((planes, tokens, width), half),
            pltpu.VMEM((planes, tokens, width), half),
            pltpu.VMEM((2, width, units), half),
            pltpu.VMEM((2, units // 2, width), half),
            pltpu.VMEM((slots, width), half),
            pltpu.VMEM((2 * slots, width), half),
            pltpu.VMEM((2 * slots, PLANE * tokens), half),
            pltpu.SemaphoreType.DMA((12, planes)),
            pltpu.SemaphoreType.DMA((12, planes)),
            pltpu.SemaphoreType.DMA((4,)),
        ],
        compiler_params=pltpu.CompilerParams(
            collective_id=0, has_side_effects=True, vmem_limit_bytes=VMEM_MOST
        ),
        name="expert_sums",
    )(x, slot, weight, up_mine, up_other, down_mine, down_other)


def weights_by_chip(routes, route_weights):
    peers, cores = lax.axis_size("ctx"), lax.axis_size("head")
    experts = jnp.arange(peers * cores, dtype=jnp.int32)
    named = (routes[None] == experts[:, None, None]).astype(jnp.float32)
    dense = jnp.sum(named * route_weights[None], axis=2).astype(jnp.bfloat16)
    dense = dense.reshape(peers, cores, routes.shape[0])
    return jnp.pad(dense, ((0, 0), (0, 16 - cores), (0, 0)))


def route_tables(seen):
    peers, cores = lax.axis_size("ctx"), lax.axis_size("head")
    tokens = seen.shape[2]
    seen = seen[:, :cores].astype(jnp.float32)
    seen = jnp.where(lax.axis_index("head") == 0, seen, seen[:, ::-1])
    seen = seen.reshape(peers // PLANE, PLANE, cores, tokens).swapaxes(1, 2)
    seen = seen.reshape(peers // PLANE, cores, PLANE * tokens)
    filled = seen > 0
    span = PLANE * tokens
    upto = (
        lax.broadcasted_iota(jnp.int32, (span, span), 0)
        <= lax.broadcasted_iota(jnp.int32, (span, span), 1)
    ).astype(jnp.bfloat16)
    rank = jnp.dot(
        filled.reshape(-1, span).astype(jnp.bfloat16), upto, preferred_element_type=jnp.float32
    ).reshape(seen.shape)
    return jnp.where(filled, rank.astype(jnp.int32) - 1, -1), seen


def post_norm(hidden, post_gain):
    hidden_full = hidden.astype(jnp.float32)
    square_mean = jnp.mean(hidden_full * hidden_full, axis=-1, keepdims=True)
    return (hidden_full / jnp.sqrt(square_mean + 1e-06) * post_gain).astype(jnp.bfloat16)


def per_device(
    pair_raw,
    value_raw,
    gate_raw,
    write_strength,
    log_decay,
    segment_ids,
    pair_filter,
    value_filter,
    norm_gain,
    out_weight,
    residual,
    post_gain,
    routes,
    route_weights,
    expert_up,
    expert_down,
):
    swap = [(0, 1), (1, 0)]
    devices_all = lax.axis_size("ctx") * lax.axis_size("head")
    up_other = lax.ppermute(expert_up, "head", swap)
    down_other = lax.ppermute(expert_down, "head", swap)
    partial, seen = mixer(
        pair_raw, value_raw, gate_raw, write_strength, log_decay, segment_ids,
        pair_filter, value_filter, norm_gain, out_weight,
        weights_by_chip(routes, route_weights),
    )
    slot, weight = route_tables(seen)
    half = partial.shape[0] // 2
    core = lax.axis_index("head")
    mine = lax.dynamic_slice_in_dim(partial, core * half, half)
    theirs = lax.dynamic_slice_in_dim(partial, (1 - core) * half, half).astype(jnp.bfloat16)
    attention = mine + lax.ppermute(theirs, "head", swap).astype(jnp.float32)
    hidden = (residual.astype(jnp.float32) + attention).astype(jnp.bfloat16)
    expert_in = post_norm(hidden, post_gain)
    capacity = routes.shape[0] * routes.shape[1] * 5 // (4 * devices_all)
    answered = expert_sums(
        expert_in, slot, weight, expert_up, up_other, expert_down, down_other, capacity
    )
    return (hidden.astype(jnp.float32) + answered).astype(jnp.bfloat16)


def solution(mesh):
    return jax.shard_map(
        per_device,
        mesh=mesh,
        in_specs=(
            P(("group", "ctx"), None, "head"),
            P(("group", "ctx"), "head"),
            P(("group", "ctx"), "head"),
            P(("group", "ctx"), "head"),
            P(("group", "ctx"), "head"),
            P("group"),
            P(None, None, "head"),
            P(None, "head"),
            P(),
            P("head", None),
            P(("group", "ctx", "head"), None),
            P(),
            P(("group", "ctx", "head"), None),
            P(("group", "ctx", "head"), None),
            P(("ctx", "head"), None, None),
            P(("ctx", "head"), None, None),
        ),
        out_specs=P(("group", "ctx", "head"), None),
        check_vma=False,
    )
```

```python
import functools

import jax
import jax.numpy as jnp
from jax import lax
from jax.experimental import pallas as pl
from jax.experimental.pallas import tpu as pltpu
from jax.sharding import PartitionSpec as P

DK = 128
DV = 128
PAD = 16
EPS = 1e-06
NN = (((1,), (0,)), ((), ()))
NT = (((1,), (1,)), ((), ()))
TN = (((0,), (0,)), ((), ()))
VMEM_MOST = 56 * 1024 * 1024


def dot16(left, right, dims=NN):
    return lax.dot_general(
        left.astype(jnp.bfloat16),
        right.astype(jnp.bfloat16),
        dims,
        preferred_element_type=jnp.float32,
    )


def halves(x):
    high = x.astype(jnp.bfloat16)
    return high, (x - high.astype(jnp.float32)).astype(jnp.bfloat16)


def dot_split(left, right, dims=NN):
    lh, ll = halves(left)
    rh, rl = halves(right)
    return dot16(lh, rh, dims) + (dot16(lh, rl, dims) + dot16(ll, rh, dims))


def silu(x):
    return x * (1.0 / (1.0 + jnp.exp(-x)))


def filtered(raw_ref, taps_ref, match, lanes):
    rows = raw_ref.shape[0] - PAD
    source = raw_ref[:, lanes].astype(jnp.float32)
    taps = taps_ref[:, lanes]
    total = taps[0:1] * source[PAD:]
    for lag in range(1, taps_ref.shape[0]):
        total = total + taps[lag : lag + 1] * (source[PAD - lag : PAD - lag + rows] * match[lag])
    return silu(total)


def unit_rows(x):
    return x * lax.rsqrt(jnp.sum(x * x, axis=-1, keepdims=True) + EPS)


def inverses_unit_lower(couplings, row, col):
    size = couplings[0].shape[0]
    apart = row ^ col
    eye = jnp.where(row == col, 1.0, 0.0)
    found = [eye - jnp.where(apart == 1, c, 0.0) for c in couplings]
    step = 2
    while step < size:
        band = (apart >= step) & (apart < 2 * step)
        crosses = [jnp.where(band, c, 0.0) for c in couplings]
        found16 = [f.astype(jnp.bfloat16) for f in found]
        inner = [dot16(c, f) for c, f in zip(crosses, found16)]
        found = [f - dot16(f16, i) for f, f16, i in zip(found, found16, inner)]
        step *= 2
    return found


def local_kernel(
    q_ref, k_ref, v_ref, qt_ref, kt_ref, vt_ref, seg_ref, segrow_ref,
    cum_ref, cumrow_ref, beta_ref, table_ref, qeff_ref, off_ref, maps_ref,
):
    rows = qeff_ref.shape[1]
    maps_ref[:, DK + DV // 2 :, :] = table_ref[...]
    seg = seg_ref[...]
    match = [None] + [(seg[:, lag : lag + 1] == seg[:, 0:1]).astype(jnp.float32) for lag in range(1, 4)]
    ids = seg[:, 0:1]
    carried = (ids == seg_ref[0:1, 1:2]).astype(jnp.float32)
    at_end = (ids == seg_ref[rows - 1 : rows, 0:1]).astype(jnp.float32)
    row = lax.broadcasted_iota(jnp.int32, (rows, rows), 0)
    col = lax.broadcasted_iota(jnp.int32, (rows, rows), 1)
    same = ids == segrow_ref[...]
    causal = (row >= col) & same
    strictly = (row > col) & same
    queries = unit_rows(filtered(q_ref, qt_ref, match, slice(None))) * DK ** (-0.5)
    keys = unit_rows(filtered(k_ref, kt_ref, match, slice(None)))
    q16 = queries.astype(jnp.bfloat16)
    k16 = keys.astype(jnp.bfloat16)
    gram = dot16(k16, k16, NT)
    cross = dot16(q16, k16, NT)
    k32 = k16.astype(jnp.float32)
    q32 = q16.astype(jnp.float32)
    eye = (
        lax.broadcasted_iota(jnp.int32, (DK, DK), 0) == lax.broadcasted_iota(jnp.int32, (DK, DK), 1)
    ).astype(jnp.float32)
    decays = [
        jnp.exp(jnp.where(causal, cum_ref[member] - cumrow_ref[member], 0.0))
        for member in range(qeff_ref.shape[0])
    ]
    found = inverses_unit_lower(
        [
            jnp.where(strictly, gram * decay * beta_ref[member], 0.0)
            for member, decay in enumerate(decays)
        ],
        row,
        col,
    )
    for member, decay in enumerate(decays):
        lanes = slice(member * DV, (member + 1) * DV)
        values = filtered(v_ref, vt_ref, match, lanes)
        cum = cum_ref[member]
        beta = beta_ref[member]
        within = jnp.where(causal, cross * decay, 0.0)
        grown = jnp.exp(cum) * carried
        stacked = jnp.concatenate([values * beta, k32 * (beta * grown)], axis=1)
        solved = dot16(found[member], stacked)
        both = dot16(within, solved)
        off_ref[member] = both[:, :DV]
        qeff_ref[member] = (q32 * grown - both[:, DV:]).astype(jnp.bfloat16)
        final = cum[rows - 1 : rows]
        weighted = k32 * (at_end * jnp.exp(final - cum))
        sums = dot16(solved, weighted, TN)
        shift_t = sums[:DV]
        forward = (jnp.exp(final) * carried[rows - 1 : rows]) * eye - sums[DV:].T
        for half in range(2):
            at = member * 2 + half
            maps_ref[at, :DK, :] = forward.astype(jnp.bfloat16)
            maps_ref[at, DK : DK + DV // 2, :] = shift_t[half * (DV // 2) : (half + 1) * (DV // 2)].astype(jnp.bfloat16)


def local_maps(pair, value, pair_taps, value_taps, seg, segrow, cum, cumrow, beta, table):
    heads, rows = beta.shape[:2]
    key_heads = pair.shape[1] // (2 * DK)
    per = heads // key_heads
    extra = table.shape[1]
    padded = pair.shape[0]
    taps = pair_taps.shape[0]
    whole = lambda g: (0, 0)
    return pl.pallas_call(
        local_kernel,
        grid=(key_heads,),
        in_specs=[
            pl.BlockSpec((padded, DK), lambda g: (0, g)),
            pl.BlockSpec((padded, DK), lambda g: (0, key_heads + g)),
            pl.BlockSpec((padded, per * DV), lambda g: (0, g)),
            pl.BlockSpec((taps, DK), lambda g: (0, g)),
            pl.BlockSpec((taps, DK), lambda g: (0, key_heads + g)),
            pl.BlockSpec((taps, per * DV), lambda g: (0, g)),
            pl.BlockSpec((rows, taps), whole),
            pl.BlockSpec((1, rows), whole),
            pl.BlockSpec((per, rows, 1), lambda g: (g, 0, 0)),
            pl.BlockSpec((per, 1, rows), lambda g: (g, 0, 0)),
            pl.BlockSpec((per, rows, 1), lambda g: (g, 0, 0)),
            pl.BlockSpec((2 * per, extra, DK), lambda g: (g, 0, 0)),
        ],
        out_specs=[
            pl.BlockSpec((per, rows, DK), lambda g: (g, 0, 0)),
            pl.BlockSpec((per, rows, DV), lambda g: (g, 0, 0)),
            pl.BlockSpec((2 * per, DK + DV // 2 + extra, DK), lambda g: (g, 0, 0)),
        ],
        out_shape=[
            jax.ShapeDtypeStruct((heads, rows, DK), jnp.bfloat16),
            jax.ShapeDtypeStruct((heads, rows, DV), jnp.float32),
            jax.ShapeDtypeStruct((2 * heads, DK + DV // 2 + extra, DK), jnp.bfloat16),
        ],
        compiler_params=pltpu.CompilerParams(vmem_limit_bytes=VMEM_MOST),
        name="local_maps",
    )(pair, pair, value, pair_taps, pair_taps, value_taps, seg, segrow, cum, cumrow, beta, table)


def carry_kernel(maps_ref, states_ref):
    state = jnp.zeros(states_ref.shape[1:], jnp.float32)
    for at in range(maps_ref.shape[0]):
        states_ref[at] = state.astype(jnp.bfloat16)
        if at + 1 < maps_ref.shape[0]:
            moved = dot16(state, maps_ref[at, :DK, :], NT)
            state = moved + maps_ref[at, DK : DK + DV // 2, :].astype(jnp.float32)


def carried_states(maps):
    peers = maps.shape[0]
    return pl.pallas_call(
        carry_kernel,
        out_shape=jax.ShapeDtypeStruct((peers, DV // 2, DK), jnp.bfloat16),
        compiler_params=pltpu.CompilerParams(vmem_limit_bytes=VMEM_MOST),
        name="carried_states",
    )(maps)


def emit_kernel(qeff_ref, off_ref, state_ref, gate_ref, gain_ref, weight_ref, out_ref, gated_ref):
    heads = qeff_ref.shape[0]
    gain = gain_ref[...]
    for head in range(heads):
        lanes = slice(head * DV, (head + 1) * DV)
        mixed = off_ref[head] + dot16(qeff_ref[head], state_ref[head], NT)
        scale = lax.rsqrt(jnp.mean(mixed * mixed, axis=-1, keepdims=True) + EPS)
        gate = silu(gate_ref[:, lanes].astype(jnp.float32))
        gated_ref[:, lanes] = (mixed * scale * gain * gate).astype(jnp.bfloat16)
    width = out_ref.shape[1]
    tile = 512
    for at in range(0, width, tile):
        out_ref[:, at : at + tile] = jnp.dot(
            gated_ref[...], weight_ref[:, at : at + tile], preferred_element_type=jnp.float32
        )


def emitted_rows(qeff, off, states, gate_raw, gain, weight):
    rows, channels = gate_raw.shape
    return pl.pallas_call(
        emit_kernel,
        out_shape=jax.ShapeDtypeStruct((rows, weight.shape[1]), jnp.float32),
        scratch_shapes=[pltpu.VMEM((rows, channels), jnp.bfloat16)],
        compiler_params=pltpu.CompilerParams(vmem_limit_bytes=VMEM_MOST),
        name="emitted_rows",
    )(qeff, off, states, gate_raw, gain, weight)


def mixer(
    pair_raw, value_raw, gate_raw, write_strength, log_decay, segment_ids,
    pair_filter, value_filter, norm_gain, out_weight, table,
):
    rows = pair_raw.shape[0]
    taps = value_filter.shape[0]
    peers = lax.axis_size("ctx")
    pair = pair_raw.reshape(rows, -1)
    width = pair.shape[1]
    rim = jnp.concatenate([pair[rows - PAD :], value_raw[rows - PAD :]], axis=1)
    before = lax.ppermute(rim, "ctx", [(i, i + 1) for i in range(peers - 1)])
    first = lax.axis_index("ctx") * rows
    padded_ids = jnp.concatenate([jnp.full((taps - 1,), -1, jnp.int32), segment_ids])
    ids = lax.dynamic_slice_in_dim(padded_ids, first, rows + taps - 1)
    seg = jnp.stack([ids[taps - 1 - lag : taps - 1 - lag + rows] for lag in range(taps)], axis=1)
    segrow = ids[taps - 1 :][None, :]
    cum = jnp.cumsum(log_decay, axis=0).T
    qeff, off, maps = local_maps(
        jnp.concatenate([before[:, :width], pair]),
        jnp.concatenate([before[:, width:], value_raw]),
        pair_filter.reshape(taps, -1),
        value_filter,
        seg,
        segrow,
        cum[:, :, None],
        cum[:, None, :],
        write_strength.T[:, :, None],
        table,
    )
    heads = qeff.shape[0]
    arrived = lax.all_to_all(maps, "ctx", split_axis=0, concat_axis=0, tiled=True)
    states = lax.all_to_all(carried_states(arrived), "ctx", split_axis=0, concat_axis=0, tiled=True)
    states = states.reshape(heads, DV, DK)
    partial = emitted_rows(qeff, off, states, gate_raw, norm_gain[None, :], out_weight)
    return partial, arrived[:, DK + DV // 2 :]

PLANE = 4
AGZ, AGX, AGY, AGA, AGB, DA, DB, XA, XB, YA, YB, RSZ = range(12)


def expert_kernel(
    x_ref, slot_ref, weight_ref, up_mine, up_other, down_mine, down_other, out_ref,
    got, part, diag, from_x, from_y, sums, from_z, up, down, rows_in, rows_out, chosen,
    send_sem, recv_sem, local_sem,
):
    planes = got.shape[0] // PLANE
    tokens = got.shape[1]
    half = tokens // 2
    first, second = pl.ds(0, half), pl.ds(half, half)
    slots = rows_in.shape[0]
    me = lax.axis_index("ctx")
    x, y, z = me % 2, (me // 2) % 2, me // PLANE
    beside_x = me + 1 - 2 * x
    beside_y = me + 2 - 4 * y

    def plane_of(k):
        return (z % 2 + k % 2) % 2 + 2 * ((z // 2 + k // 2) % 2)

    def along_z(k):
        return PLANE * plane_of(k) + 2 * y + x

    def block(k, flip_y, flip_x):
        row = 1 - y if flip_y else y
        column = 1 - x if flip_x else x
        return PLANE * plane_of(k) + 2 * row + column

    def copy(kind, k, source, target, device):
        return pltpu.make_async_remote_copy(
            src_ref=source,
            dst_ref=target,
            send_sem=send_sem.at[kind, k],
            recv_sem=recv_sem.at[kind, k],
            device_id={"ctx": device},
            device_id_type=pl.DeviceIdType.MESH,
        )

    def arrived(kind, k, place, device):
        copy(kind, k, place, place, device).wait_recv()

    loads = [
        pltpu.make_async_copy(source, target, local_sem.at[at])
        for at, (source, target) in enumerate(
            [
                (up_mine.at[0], up.at[0]),
                (up_other.at[0], up.at[1]),
                (down_mine.at[0], down.at[0]),
                (down_other.at[0], down.at[1]),
            ]
        )
    ]
    for load in loads:
        load.start()
    got[me] = x_ref[...]

    partners = [beside_x, beside_y] + [along_z(k) for k in range(1, planes)]
    barrier = pltpu.get_barrier_semaphore()
    for partner in partners:
        pl.semaphore_signal(
            barrier, inc=1, device_id={"ctx": partner}, device_id_type=pl.DeviceIdType.MESH
        )
    pl.semaphore_wait(barrier, len(partners))

    def share_in_plane(k):
        own = block(k, False, False)
        copy(AGX, k, got.at[own], got.at[own], beside_x).start()
        copy(AGY, k, got.at[own], got.at[own], beside_y).start()

    def share_along_z(k):
        copy(AGZ, k, got.at[me], got.at[me], along_z(k)).start()

    def pass_on(k):
        across_x, across_y = block(k, False, True), block(k, True, False)
        arrived(AGX, k, got.at[across_x], beside_x)
        copy(AGA, k, got.at[across_x, first], got.at[across_x, first], beside_y).start()
        arrived(AGY, k, got.at[across_y], beside_y)
        copy(AGB, k, got.at[across_y, second], got.at[across_y, second], beside_x).start()

    def take_from_z(k):
        arrived(AGZ, k, got.at[along_z(k)], along_z(k))
        share_in_plane(k)

    share_in_plane(0)
    share_along_z(1)
    pass_on(0)
    share_along_z(2)
    take_from_z(1)
    for load in loads:
        load.wait()

    def experts(k):
        plane = plane_of(k)
        base = PLANE * plane
        slot_rows = slot_ref[plane]
        weight_rows = weight_ref[plane]
        place = lax.broadcasted_iota(jnp.int32, (slots, PLANE * tokens), 0)
        source = got[pl.ds(base, PLANE)].reshape(PLANE * tokens, got.shape[2])
        for e in range(2):
            here = place == slot_rows[e : e + 1]
            pick = jnp.where(here, 1.0, 0.0).astype(jnp.bfloat16)
            chosen[pl.ds(e * slots, slots), :] = jnp.where(here, weight_rows[e : e + 1], 0.0).astype(
                jnp.bfloat16
            )
            rows_in[...] = jnp.dot(pick, source, preferred_element_type=jnp.float32).astype(
                jnp.bfloat16
            )
            units = jnp.dot(rows_in[...], up[e], preferred_element_type=jnp.float32)
            width = units.shape[1] // 2
            active = (silu(units[:, :width]) * units[:, width:]).astype(jnp.bfloat16)
            rows_out[pl.ds(e * slots, slots), :] = jnp.dot(
                active, down[e], preferred_element_type=jnp.float32
            ).astype(jnp.bfloat16)
        for b in range(PLANE):
            part[base + b] = lax.dot_general(
                chosen[:, b * tokens : (b + 1) * tokens],
                rows_out[...],
                TN,
                preferred_element_type=jnp.float32,
            ).astype(jnp.bfloat16)

    def give_first(k):
        across, xb, yb = block(k, True, True), block(k, False, True), block(k, True, False)
        copy(DA, k, part.at[across, first], diag.at[k, first], beside_y).start()
        copy(DB, k, part.at[across, second], diag.at[k, second], beside_x).start()
        copy(XB, k, part.at[xb, second], from_x.at[k, second], beside_x).start()
        copy(YA, k, part.at[yb, first], from_y.at[k, first], beside_y).start()

    def give_second(k):
        xb, yb = block(k, False, True), block(k, True, False)
        arrived(DA, k, diag.at[k, first], beside_y)
        part[xb, first] = (
            part[xb, first].astype(jnp.float32) + diag[k, first].astype(jnp.float32)
        ).astype(jnp.bfloat16)
        copy(XA, k, part.at[xb, first], from_x.at[k, first], beside_x).start()
        arrived(DB, k, diag.at[k, second], beside_x)
        part[yb, second] = (
            part[yb, second].astype(jnp.float32) + diag[k, second].astype(jnp.float32)
        ).astype(jnp.bfloat16)
        copy(YB, k, part.at[yb, second], from_y.at[k, second], beside_y).start()

    def plane_sum(k):
        arrived(XA, k, from_x.at[k, first], beside_x)
        arrived(XB, k, from_x.at[k, second], beside_x)
        arrived(YA, k, from_y.at[k, first], beside_y)
        arrived(YB, k, from_y.at[k, second], beside_y)
        own = block(k, False, False)
        return (
            part[own].astype(jnp.float32)
            + from_x[k].astype(jnp.float32)
            + from_y[k].astype(jnp.float32)
        )

    def give_third(k):
        sums[k] = plane_sum(k).astype(jnp.bfloat16)
        copy(RSZ, k, sums.at[k], from_z.at[k], along_z(k)).start()

    def turn(k, unused):
        @pl.when(k < planes - 1)
        def _():
            pass_on(k + 1)

        @pl.when(k == 0)
        def _():
            share_along_z(3)
            take_from_z(2)

        across = block(k, True, True)
        arrived(AGA, k, got.at[across, first], beside_y)
        arrived(AGB, k, got.at[across, second], beside_x)
        experts(k)

        @pl.when(k >= 1)
        def _():
            give_first(k)

        @pl.when(k == 1)
        def _():
            take_from_z(3)

        @pl.when(k >= 2)
        def _():
            give_second(k - 1)

        @pl.when(k >= 3)
        def _():
            give_third(k - 2)

        return unused

    lax.fori_loop(0, planes, turn, 0)
    give_first(0)
    give_second(3)
    give_third(2)
    give_second(0)
    give_third(3)
    total = plane_sum(0)
    for k in range(1, planes):
        arrived(RSZ, k, from_z.at[k], along_z(k))
        total = total + from_z[k].astype(jnp.float32)
    out_ref[...] = total

    for k in range(planes):
        for kind in (AGX, AGY):
            copy(kind, k, got.at[0], got.at[0], beside_x).wait_send()
        for kind in (AGA, AGB):
            copy(kind, k, got.at[0, first], got.at[0, first], beside_x).wait_send()
        for kind in (DA, DB, XA, XB, YA, YB):
            copy(kind, k, part.at[0, first], diag.at[0, first], beside_x).wait_send()
        if k > 0:
            copy(AGZ, k, got.at[0], got.at[0], beside_x).wait_send()
            copy(RSZ, k, sums.at[0], from_z.at[0], beside_x).wait_send()


def expert_sums(x, slot, weight, up_mine, up_other, down_mine, down_other, capacity):
    peers = lax.axis_size("ctx")
    planes = peers // PLANE
    assert planes == 4 and x.shape[0] % 32 == 0
    tokens, width = x.shape
    units = up_mine.shape[2]
    slots = (PLANE * capacity + 15) // 16 * 16
    vmem = pl.BlockSpec(memory_space=pltpu.VMEM)
    hbm = pl.BlockSpec(memory_space=pl.ANY)
    half = jnp.bfloat16
    return pl.pallas_call(
        expert_kernel,
        out_shape=jax.ShapeDtypeStruct((tokens, width), jnp.float32),
        in_specs=[vmem, vmem, vmem, hbm, hbm, hbm, hbm],
        out_specs=vmem,
        scratch_shapes=[
            pltpu.VMEM((peers, tokens, width), half),
            pltpu.VMEM((peers, tokens, width), half),
            pltpu.VMEM((planes, tokens, width), half),
            pltpu.VMEM((planes, tokens, width), half),
            pltpu.VMEM((planes, tokens, width), half),
            pltpu.VMEM((planes, tokens, width), half),
            pltpu.VMEM((planes, tokens, width), half),
            pltpu.VMEM((2, width, units), half),
            pltpu.VMEM((2, units // 2, width), half),
            pltpu.VMEM((slots, width), half),
            pltpu.VMEM((2 * slots, width), half),
            pltpu.VMEM((2 * slots, PLANE * tokens), half),
            pltpu.SemaphoreType.DMA((12, planes)),
            pltpu.SemaphoreType.DMA((12, planes)),
            pltpu.SemaphoreType.DMA((4,)),
        ],
        compiler_params=pltpu.CompilerParams(
            collective_id=0, has_side_effects=True, vmem_limit_bytes=VMEM_MOST
        ),
        name="expert_sums",
    )(x, slot, weight, up_mine, up_other, down_mine, down_other)


def weights_by_chip(routes, route_weights):
    peers, cores = lax.axis_size("ctx"), lax.axis_size("head")
    experts = jnp.arange(peers * cores, dtype=jnp.int32)
    named = (routes[None] == experts[:, None, None]).astype(jnp.float32)
    dense = jnp.sum(named * route_weights[None], axis=2).astype(jnp.bfloat16)
    dense = dense.reshape(peers, cores, routes.shape[0])
    return jnp.pad(dense, ((0, 0), (0, 16 - cores), (0, 0)))


def route_tables(seen):
    peers, cores = lax.axis_size("ctx"), lax.axis_size("head")
    tokens = seen.shape[2]
    seen = seen[:, :cores].astype(jnp.float32)
    seen = jnp.where(lax.axis_index("head") == 0, seen, seen[:, ::-1])
    seen = seen.reshape(peers // PLANE, PLANE, cores, tokens).swapaxes(1, 2)
    seen = seen.reshape(peers // PLANE, cores, PLANE * tokens)
    filled = seen > 0
    span = PLANE * tokens
    upto = (
        lax.broadcasted_iota(jnp.int32, (span, span), 0)
        <= lax.broadcasted_iota(jnp.int32, (span, span), 1)
    ).astype(jnp.bfloat16)
    rank = jnp.dot(
        filled.reshape(-1, span).astype(jnp.bfloat16), upto, preferred_element_type=jnp.float32
    ).reshape(seen.shape)
    return jnp.where(filled, rank.astype(jnp.int32) - 1, -1), seen


def post_norm(hidden, post_gain):
    hidden_full = hidden.astype(jnp.float32)
    square_mean = jnp.mean(hidden_full * hidden_full, axis=-1, keepdims=True)
    return (hidden_full / jnp.sqrt(square_mean + 1e-06) * post_gain).astype(jnp.bfloat16)


def per_device(
    pair_raw,
    value_raw,
    gate_raw,
    write_strength,
    log_decay,
    segment_ids,
    pair_filter,
    value_filter,
    norm_gain,
    out_weight,
    residual,
    post_gain,
    routes,
    route_weights,
    expert_up,
    expert_down,
):
    swap = [(0, 1), (1, 0)]
    devices_all = lax.axis_size("ctx") * lax.axis_size("head")
    up_other = lax.ppermute(expert_up, "head", swap)
    down_other = lax.ppermute(expert_down, "head", swap)
    partial, seen = mixer(
        pair_raw, value_raw, gate_raw, write_strength, log_decay, segment_ids,
        pair_filter, value_filter, norm_gain, out_weight,
        weights_by_chip(routes, route_weights),
    )
    slot, weight = route_tables(seen)
    half = partial.shape[0] // 2
    core = lax.axis_index("head")
    mine = lax.dynamic_slice_in_dim(partial, core * half, half)
    theirs = lax.dynamic_slice_in_dim(partial, (1 - core) * half, half).astype(jnp.bfloat16)
    attention = mine + lax.ppermute(theirs, "head", swap).astype(jnp.float32)
    hidden = (residual.astype(jnp.float32) + attention).astype(jnp.bfloat16)
    expert_in = post_norm(hidden, post_gain)
    capacity = routes.shape[0] * routes.shape[1] * 5 // (4 * devices_all)
    answered = expert_sums(
        expert_in, slot, weight, expert_up, up_other, expert_down, down_other, capacity
    )
    return (hidden.astype(jnp.float32) + answered).astype(jnp.bfloat16)


def solution(mesh):
    return jax.shard_map(
        per_device,
        mesh=mesh,
        in_specs=(
            P(("group", "ctx"), None, "head"),
            P(("group", "ctx"), "head"),
            P(("group", "ctx"), "head"),
            P(("group", "ctx"), "head"),
            P(("group", "ctx"), "head"),
            P("group"),
            P(None, None, "head"),
            P(None, "head"),
            P(),
            P("head", None),
            P(("group", "ctx", "head"), None),
            P(),
            P(("group", "ctx", "head"), None),
            P(("group", "ctx", "head"), None),
            P(("ctx", "head"), None, None),
            P(("ctx", "head"), None, None),
        ),
        out_specs=P(("group", "ctx", "head"), None),
        check_vma=False,
    )
```
